128 devices in a mesh: fa: 8 (over z, x_hi), fb: 16 (over x_lo, y, core).
Axes of the slice: x: 4 (x_hi: 2, x_lo: 2; x = x_hi * 2 + x_lo), y: 4, z: 4, core: 2. Of those that a mesh axis runs over, the one named last changes fastest.
Arguments:
- view_a: bfloat16 [4096, 8192], P(('fa', 'fb')), may hold values from -300 to 300
- view_b: bfloat16 [4096, 8192], P(('fa', 'fb')), may hold values from -300 to 300
Outputs:
- loss: float32 [], replicated
- grad_a: bfloat16 [4096, 8192], P(('fa', 'fb'))
- grad_b: bfloat16 [4096, 8192], P(('fa', 'fb'))
The draws below stay inside these ranges and needn't reach their ends.
All inputs are finite; a program needn't handle non-finite values.
Results may differ from the reference program's by a relative error of at most 0.04.
Values may be sent and summed in bfloat16 or wider, within the bound.
No kernel may reach another device: no remote copies, remote signals or barrier semaphores. Data moves between devices by JAX's collectives and lax.ppermute only.
A program may use at most 192 MiB of HBM per device.

```python
import math
import jax
import jax.numpy as jnp
from jax import lax

F = 8192
BATCH = 4096
N_FA = 8
N_FB = 16


def factor_count():
    return max(F // 64, 4)


def shared_noise(key):
    first, second = jax.random.split(key)
    common = jnp.clip(jax.random.normal(first, (BATCH, F), jnp.float32), -5.0, 5.0)
    factors = jnp.clip(jax.random.normal(second, (BATCH, factor_count()), jnp.float32), -5.0, 5.0)
    return (common, factors)


def feature_spread(key):
    first, second, third, fourth = jax.random.split(key, 4)
    place = jnp.arange(F, dtype=jnp.float32) / F
    loading = jax.random.uniform(first, (2, F), jnp.float32, -1.0, 1.0) * (0.075 * (0.4 + 0.8 * place))
    scales = jnp.exp(jax.random.uniform(second, (F,), jnp.float32, 0.0, math.log(10.0)))
    shifts = 2.0 * jnp.clip(jax.random.normal(third, (F,), jnp.float32), -3.0, 3.0)
    picks = jax.random.randint(fourth, (2, F), 0, factor_count())
    return (place, loading, scales, shifts, picks)


def factor_part(factors, loading, picks):
    first = jnp.take(factors, picks[0], axis=1)
    second = jnp.take(factors, picks[1], axis=1)
    return loading[0] * first + loading[1] * second


def draw_view_a(key, part):
    common, factors = shared_noise(key)
    key = jax.random.fold_in(key, 11)
    place, loading, scales, shifts, picks = feature_spread(key)
    base = common + factor_part(factors, loading, picks)
    return (base * scales + shifts).astype(jnp.bfloat16)


def draw_view_b(key, part):
    common, factors = shared_noise(key)
    key = jax.random.fold_in(key, 23)
    place, loading, scales, shifts, picks = feature_spread(key)
    own_key = jax.random.fold_in(key, 7)
    own = jnp.clip(jax.random.normal(own_key, (BATCH, F), jnp.float32), -5.0, 5.0)
    linked = 0.94 + 0.05 * place
    base = linked * common + jnp.sqrt(1.0 - linked * linked) * own + factor_part(factors, loading, picks)
    return (base * scales + shifts).astype(jnp.bfloat16)


def setup_inputs(seed: int = 0) -> dict:
    splits = jax.random.split(jax.random.key(seed), 3)
    return {
        "view_a": draw_view_a(jax.random.fold_in(splits[2], 71), 0),
        "view_b": draw_view_b(jax.random.fold_in(splits[2], 71), 0),
    }


off_weight = 0.0051
norm_eps = 1e-05

def normalize(view):
    values = view.astype(jnp.float32)
    mean = lax.optimization_barrier(jnp.mean(values, axis=0))
    centred = values - mean
    var = lax.optimization_barrier(jnp.mean(centred * centred, axis=0))
    rstd = lax.rsqrt(var + norm_eps)
    return (centred * rstd, rstd)

def norm_backward(grads, norm_f, rstd):
    mean_g = lax.optimization_barrier(jnp.mean(grads, axis=0))
    mean_gn = lax.optimization_barrier(jnp.mean(grads * norm_f, axis=0))
    return (rstd * (grads - mean_g - norm_f * mean_gn)).astype(jnp.bfloat16)

def reference(view_a, view_b):
    width_a = F // N_FA
    width_b = F // N_FB
    norm_a, rstd_a = normalize(view_a)
    norm_b, rstd_b = normalize(view_b)
    normed_a = norm_a.astype(jnp.bfloat16)
    normed_b = norm_b.astype(jnp.bfloat16)
    a_blocks = normed_a.reshape(BATCH, N_FA, width_a).transpose(1, 0, 2)
    b_groups = normed_b.reshape(BATCH, N_FB, width_b).astype(jnp.float32)

    def step(carry, inputs):
        gb_total, loss_total = carry
        block, index = inputs
        corr = jnp.dot(block.T, normed_b, preferred_element_type=jnp.float32) / BATCH
        row_ids = index * width_a + lax.broadcasted_iota(jnp.int32, (width_a, F), 0)
        col_ids = lax.broadcasted_iota(jnp.int32, (width_a, F), 1)
        diagonal = row_ids == col_ids
        missing = 1.0 - corr
        loss_total = loss_total + jnp.sum(jnp.where(diagonal, missing * missing, off_weight * corr * corr))
        gcorr = jnp.where(diagonal, -2.0 * missing, 2.0 * off_weight * corr).astype(jnp.bfloat16)
        terms = jnp.einsum('kgj,igj->gki', b_groups, gcorr.astype(jnp.float32).reshape(width_a, N_FB, width_b), precision=lax.Precision.HIGHEST)
        terms = lax.optimization_barrier(terms.astype(jnp.bfloat16))
        ga_block = lax.optimization_barrier(jnp.sum(terms.astype(jnp.float32), axis=0))
        gb_term = jnp.dot(block, gcorr, preferred_element_type=jnp.float32)
        gb_term = lax.optimization_barrier(gb_term.astype(jnp.bfloat16))
        gb_total = gb_total + gb_term.astype(jnp.float32)
        return ((gb_total, loss_total), ga_block)
    start = (jnp.zeros((BATCH, F), jnp.float32), jnp.zeros((), jnp.float32))
    (gb_full, raw), ga_blocks = lax.scan(step, start, (a_blocks, jnp.arange(N_FA, dtype=jnp.int32)))
    ga_full = ga_blocks.transpose(1, 0, 2).reshape(BATCH, F)
    grad_a = norm_backward(ga_full, norm_a, rstd_a)
    grad_b = norm_backward(gb_full, norm_b, rstd_b)
    return (raw / F, grad_a, grad_b)
```

```python
import functools

import jax
import jax.numpy as jnp
from jax import lax
from jax.experimental import pallas as pl
from jax.experimental.pallas import tpu as pltpu
from jax.sharding import Mesh, PartitionSpec as P

off_weight = 0.0051
norm_eps = 1e-05
bf16 = jnp.bfloat16
f32 = jnp.float32
axes = ("z", "xh", "xl", "y", "c")
chips = ("z", "xh", "xl", "y")
lanes = 128


def call(kernel, out_shape, *args, scratch=(), flops=0):
    one = isinstance(out_shape, jax.ShapeDtypeStruct)
    outs = [out_shape] if one else list(out_shape)
    moved = sum(a.size * a.dtype.itemsize for a in list(args) + outs)
    vmem = pl.BlockSpec(memory_space=pltpu.VMEM)
    return pl.pallas_call(
        kernel,
        out_shape=out_shape,
        in_specs=[vmem] * len(args),
        out_specs=vmem if one else [vmem] * len(outs),
        scratch_shapes=list(scratch),
        compiler_params=pltpu.CompilerParams(vmem_limit_bytes=48 * 2**20),
        cost_estimate=pl.CostEstimate(flops=flops, bytes_accessed=moved, transcendentals=0),
    )(*args)


def shape(dims, dtype):
    return jax.ShapeDtypeStruct(dims, dtype)


def shift(x, axis, step):
    n = lax.axis_size(axis)
    return lax.ppermute(x, axis, [(i, (i + step) % n) for i in range(n)])


def swap(x, axis, bit):
    return lax.ppermute(x, axis, [(i, i ^ bit) for i in range(lax.axis_size(axis))])


def stats_kernel(x_ref, out_ref):
    x = x_ref[...].astype(f32)
    mean = jnp.mean(x, axis=0, keepdims=True)
    centred = x - mean
    m2 = jnp.sum(centred * centred, axis=0, keepdims=True)
    width = x.shape[1]
    out_ref[...] = jnp.concatenate([mean, m2, jnp.zeros((6, width), f32)], axis=0)


def merge_stats(mine, other, rows):
    delta = other[0:1] - mine[0:1]
    mean = 0.5 * (mine[0:1] + other[0:1])
    var = (mine[1:2] + other[1:2]) / (2 * rows) + 0.25 * delta * delta
    return mean, lax.rsqrt(var + norm_eps)


def norm_kernel(x_ref, mine_ref, other_ref, a_ref, b_ref, diag_ref):
    rows = x_ref.shape[0]
    mean, rstd = merge_stats(mine_ref[...], other_ref[...], rows)
    norm = ((x_ref[...].astype(f32) - mean) * rstd).astype(bf16)
    a = norm[:, :lanes]
    b = norm[:, lanes:]
    a_ref[...] = a
    b_ref[...] = b
    diag = jnp.sum(a.astype(f32) * b.astype(f32), axis=0, keepdims=True)
    diag_ref[...] = jnp.broadcast_to(diag, diag_ref.shape)


def corr_kernel(*refs):
    a, b, out_ref, a_t = refs[:8], refs[8:16], refs[16], refs[17]
    rows = a[0].shape[0]
    for i in range(8):
        a_t[i * lanes : (i + 1) * lanes, :] = a[i][...].T
    for q in range(4):
        right = jnp.concatenate([b[2 * q][...], b[2 * q + 1][...]], axis=1)
        for p in range(4):
            here = pl.ds(p * 256, 256)
            out_ref[here, q * 256 : (q + 1) * 256] = jnp.dot(
                a_t[here, :], right, preferred_element_type=f32
            ).astype(bf16)


def grad_blocks(b, g_ref, outs, pair, transposed):
    rows = b[0].shape[0]
    cols = slice(pair * 256, (pair + 1) * 256)
    step = 256
    for r in range(0, rows, step):
        left = jnp.concatenate([v[r : r + step, :] for v in b], axis=1)
        if transposed:
            out = lax.dot_general(
                left, g_ref[cols, :], (((1,), (1,)), ((), ())), preferred_element_type=f32
            )
        else:
            out = jnp.dot(left, g_ref[:, cols], preferred_element_type=f32)
        out = out.astype(bf16)
        outs[0][r : r + step, :] = out[:, :lanes]
        outs[1][r : r + step, :] = out[:, lanes:]


def first_kernel(batch, *refs):
    a, b = refs[:8], refs[8:16]
    mine, other, diag_mine, diag_other = refs[16:20]
    g_ref, loss_ref, diag_ref = refs[20:23]
    ga, gb = refs[23:25], refs[25:27]
    size = mine.shape[0]
    diag = (diag_mine[...] + diag_other[...]) / batch
    diag_ref[...] = diag
    first = lax.broadcasted_iota(jnp.int32, (8, lanes), 0) == 0
    missing = 1.0 - diag
    total = jnp.where(first, missing * missing, 0.0)
    step = 128
    for r in range(0, size, step):
        corr = (mine[r : r + step, :].astype(f32) + other[r : r + step, :].astype(f32)) / batch
        if r == 0:
            ids = lax.broadcasted_iota(jnp.int32, (step, size), 0)
            corr = jnp.where(ids == lax.broadcasted_iota(jnp.int32, (step, size), 1), 0.0, corr)
        g_ref[r : r + step, :] = (2.0 * off_weight * corr).astype(bf16)
        square = jnp.sum((off_weight * corr * corr).reshape(step // 8, 8, size), axis=0)
        total = total + sum(square[:, c : c + lanes] for c in range(0, size, lanes))
    loss_ref[...] = total
    grad_blocks(b, g_ref, ga, 3, True)
    grad_blocks(a, g_ref, gb, 3, False)


def rest_kernel(*refs):
    a, b, g_ref = refs[:8], refs[8:16], refs[16]
    outs = refs[17:]
    ga, gb = outs[:6], outs[6:]
    for pair in (2, 1, 0):
        grad_blocks(b, g_ref, ga[2 * pair : 2 * pair + 2], pair, True)
        grad_blocks(a, g_ref, gb[2 * pair : 2 * pair + 2], pair, False)


def add_kernel(*refs):
    n = len(refs) // 3
    for i in range(n):
        x, y, out = refs[2 * i], refs[2 * i + 1], refs[2 * n + i]
        out[...] = (x[...].astype(f32) + y[...].astype(f32)).astype(bf16)


def add3_kernel(*refs):
    n = len(refs) // 4
    for i in range(n):
        x, y, z, out = refs[3 * i], refs[3 * i + 1], refs[3 * i + 2], refs[3 * n + i]
        out[...] = (x[...].astype(f32) + y[...].astype(f32) + z[...].astype(f32)).astype(bf16)


def sums_kernel(x_ref, mine_ref, other_ref, diag_ref, *refs):
    parts_a, parts_b = refs[:4], refs[4:8]
    full_ref, sums_ref = refs[8:]
    rows = x_ref.shape[0]
    mean, rstd = merge_stats(mine_ref[...], other_ref[...], rows)
    norm = (x_ref[...].astype(f32) - mean) * rstd
    rounded = norm.astype(bf16).astype(f32)
    coef = -2.0 * (1.0 - diag_ref[0:1, :])
    ga = sum(p[...].astype(f32) for p in parts_a) + coef * rounded[:, lanes:]
    gb = sum(p[...].astype(f32) for p in parts_b) + coef * rounded[:, :lanes]
    full = jnp.concatenate([ga, gb], axis=1)
    full_ref[...] = full
    s1 = jnp.sum(full, axis=0, keepdims=True)
    s2 = jnp.sum(full * norm, axis=0, keepdims=True)
    sums_ref[...] = jnp.concatenate([s1, s2, jnp.zeros((6, 2 * lanes), f32)], axis=0)


def final_kernel(x_ref, mine_ref, other_ref, full_ref, s_mine, s_other, out_ref):
    rows = x_ref.shape[0]
    mean, rstd = merge_stats(mine_ref[...], other_ref[...], rows)
    norm = (x_ref[...].astype(f32) - mean) * rstd
    sums = (s_mine[...] + s_other[...]) / (2 * rows)
    out_ref[...] = (rstd * (full_ref[...] - sums[0:1] - norm * sums[1:2])).astype(bf16)


def gather(own, ring, pair):
    across = shift(own, pair, 1)
    left = shift(own, ring, 1)
    right = shift(own, ring, -1)
    across_left = shift(across, ring, 1)
    opposite = shift(right, ring, -1)
    across_right = shift(across, ring, -1)
    across_opposite = shift(across_left, ring, 1)
    return [own, across, left, across_left, right, across_right, opposite, across_opposite]


def on_device(view_a, view_b):
    rows_dev, features = view_a.shape
    groups = features // lanes
    rows = rows_dev * groups
    batch = 2 * rows
    block = shape((rows, lanes), bf16)

    def split(view):
        return view.reshape(rows_dev, groups, lanes).transpose(1, 0, 2)

    both = jnp.concatenate([split(view_a), split(view_b)], axis=2)
    x = lax.all_to_all(both, chips, 0, 0, tiled=True).reshape(rows, 2 * lanes)
    mine = call(stats_kernel, shape((8, 2 * lanes), f32), x)
    other = shift(mine, "c", 1)
    own_a, own_b, diag_mine = call(
        norm_kernel, (block, block, shape((8, lanes), f32)), x, mine, other
    )
    diag_other = shift(diag_mine, "c", 1)
    a = gather(own_a, "y", "xl")
    b = gather(own_b, "z", "xh")
    size = 8 * lanes
    work = 2 * rows * size * size
    corr_mine = call(
        corr_kernel,
        shape((size, size), bf16),
        *a,
        *b,
        scratch=[pltpu.VMEM((size, rows), bf16)],
        flops=work,
    )
    corr_other = shift(corr_mine, "c", 1)
    g, loss, diag, a_o, a_xo, b_o, b_xo = call(
        functools.partial(first_kernel, batch),
        (shape((size, size), bf16), shape((8, lanes), f32), shape((8, lanes), f32))
        + (block,) * 4,
        *a,
        *b,
        corr_mine,
        corr_other,
        diag_mine,
        diag_other,
        flops=work // 2,
    )
    a_r1, a_r2 = shift(a_o, "y", 1), shift(a_xo, "y", -1)
    b_r1, b_r2 = shift(b_o, "z", 1), shift(b_xo, "z", -1)
    rest = call(rest_kernel, (block,) * 12, *a, *b, g, flops=work * 3 // 2)
    a_p, a_q, a_l, a_xl, a_r, a_xr = rest[:6]
    b_p, b_q, b_l, b_xl, b_r, b_xr = rest[6:]
    a_xr_in, b_xr_in = shift(a_xr, "y", 1), shift(b_xr, "z", 1)
    a_xl, b_xl = call(add_kernel, (block,) * 2, a_xl, a_r2, b_xl, b_r2)
    a_xl_in, b_xl_in = shift(a_xl, "y", -1), shift(b_xl, "z", -1)
    a_r, b_r = call(add_kernel, (block,) * 2, a_r, a_r1, b_r, b_r1)
    a_r_in, b_r_in = shift(a_r, "y", 1), shift(b_r, "z", 1)
    a_l_in, b_l_in = shift(a_l, "y", -1), shift(b_l, "z", -1)
    a_q, b_q = call(add3_kernel, (block,) * 2, a_q, a_xr_in, a_xl_in, b_q, b_xr_in, b_xl_in)
    a_q_in, b_q_in = shift(a_q, "xl", 1), shift(b_q, "xh", 1)
    full, s_mine = call(
        sums_kernel,
        (shape((rows, 2 * lanes), f32), shape((8, 2 * lanes), f32)),
        x,
        mine,
        other,
        diag,
        a_p,
        a_r_in,
        a_l_in,
        a_q_in,
        b_p,
        b_r_in,
        b_l_in,
        b_q_in,
    )
    s_other = shift(s_mine, "c", 1)
    out = call(
        final_kernel, shape((rows, 2 * lanes), bf16), x, mine, other, full, s_mine, s_other
    )
    back = lax.all_to_all(out.reshape(groups, rows_dev, 2 * lanes), chips, 0, 0, tiled=True)
    grad_a = back[:, :, :lanes].transpose(1, 0, 2).reshape(rows_dev, features)
    grad_b = back[:, :, lanes:].transpose(1, 0, 2).reshape(rows_dev, features)
    for axis, bit in (("xl", 1), ("xh", 1), ("y", 1), ("y", 2), ("z", 1), ("z", 2)):
        loss = loss + swap(loss, axis, bit)
    return (jnp.sum(loss) / features, grad_a, grad_b)


def solution(mesh):
    split = Mesh(mesh.devices.reshape(4, 2, 2, 4, 2), axes)
    return jax.shard_map(
        on_device,
        mesh=split,
        in_specs=(P(axes, None), P(axes, None)),
        out_specs=(P(), P(axes, None), P(axes, None)),
        check_vma=False,
    )
```

```python
import functools

import jax
import jax.numpy as jnp
from jax import lax
from jax.experimental import pallas as pl
from jax.experimental.pallas import tpu as pltpu
from jax.sharding import Mesh, PartitionSpec as P

off_weight = 0.0051
norm_eps = 1e-05
bf16 = jnp.bfloat16
f32 = jnp.float32
axes = ("z", "x", "y", "c")
chips = ("z", "x", "y")
sizes = (4, 4, 4, 2)
lanes = 128
vmem_limit = 40 * 2**20
half = 2048
loss_rows = 8


def call(kernel, out_shape, *args, scratch=(), flops=0, scalar=False):
    one = isinstance(out_shape, jax.ShapeDtypeStruct)
    outs = [out_shape] if one else list(out_shape)
    vmem = pl.BlockSpec(memory_space=pltpu.VMEM)
    specs = [vmem] * len(args)
    if scalar:
        specs[0] = pl.BlockSpec(memory_space=pltpu.SMEM)
    traffic = sum(a.size * a.dtype.itemsize for a in list(args) + outs)
    return pl.pallas_call(
        kernel,
        out_shape=out_shape,
        in_specs=specs,
        out_specs=vmem if one else [vmem] * len(outs),
        scratch_shapes=list(scratch),
        compiler_params=pltpu.CompilerParams(vmem_limit_bytes=vmem_limit),
        cost_estimate=pl.CostEstimate(flops=flops, bytes_accessed=traffic, transcendentals=0),
    )(*args)


def shape(dims, dtype):
    return jax.ShapeDtypeStruct(dims, dtype)


def device(z, x, y, c):
    return ((z * 4 + x) * 4 + y) * 2 + c


def moved(target):
    places = [(z, x, y, c) for z in range(4) for x in range(4) for y in range(4) for c in range(2)]
    return [(device(*p), device(*target(*p))) for p in places]


def line(x, role, step):
    def target(z, x, y, c):
        return (z, x, (y + step) % 4, c) if c == role else ((z + step) % 4, x, y, c)

    return lax.ppermute(x, axes, moved(target))


def across(x, role):
    def target(z, x, y, c):
        return (z, x ^ 1 if c == role else 3 - x, y, c)

    return lax.ppermute(x, axes, moved(target))


def swap(x):
    return lax.ppermute(x, axes, moved(lambda z, x, y, c: (z, x, y, 1 - c)))


def gate(*xs):
    hbm = pl.BlockSpec(memory_space=pltpu.HBM)
    return pl.pallas_call(
        lambda *refs: None,
        out_shape=[shape(x.shape, x.dtype) for x in xs],
        in_specs=[hbm] * len(xs),
        out_specs=[hbm] * len(xs),
        input_output_aliases={n: n for n in range(len(xs))},
    )(*xs)


def stats_kernel(x_ref, out_ref):
    x = x_ref[...].astype(f32)
    mean = jnp.mean(x, axis=0, keepdims=True)
    centred = x - mean
    m2 = jnp.sum(centred * centred, axis=0, keepdims=True)
    width = x.shape[1]
    out_ref[...] = jnp.concatenate([mean, m2, jnp.zeros((6, width), f32)], axis=0)


def merge_stats(mine, other, rows):
    other = jnp.concatenate([other[:, lanes:], other[:, :lanes]], axis=1)
    delta = other[0:1] - mine[0:1]
    mean = 0.5 * (mine[0:1] + other[0:1])
    var = (mine[1:2] + other[1:2]) / (2 * rows) + 0.25 * delta * delta
    return mean, lax.rsqrt(var + norm_eps)


def norm_kernel(x_ref, mine_ref, other_ref, a_ref, b_ref, diag_ref):
    rows = x_ref.shape[0]
    mean, rstd = merge_stats(mine_ref[...], other_ref[...], rows)
    norm = ((x_ref[...].astype(f32) - mean) * rstd).astype(bf16)
    a = norm[:, :lanes]
    b = norm[:, lanes:]
    a_ref[...] = a
    b_ref[...] = b
    diag = jnp.sum(a.astype(f32) * b.astype(f32), axis=0, keepdims=True)
    diag_ref[...] = jnp.broadcast_to(diag, diag_ref.shape)


def by_core(core_ref, body, first, second):
    @pl.when(core_ref[0] == 0)
    def _():
        body(first, second)

    @pl.when(core_ref[0] != 0)
    def _():
        body(second, first)


def corr_kernel(core_ref, *refs):
    first, second, out_ref, a_t = refs[:8], refs[8:16], refs[16], refs[17]

    def body(a, b):
        for i in range(8):
            a_t[i * lanes : (i + 1) * lanes, :] = a[i][...].T
        for q in range(4):
            right = jnp.concatenate([b[2 * q][...], b[2 * q + 1][...]], axis=1)
            for p in range(4):
                here = pl.ds(p * 256, 256)
                out_ref[here, q * 256 : (q + 1) * 256] = jnp.dot(
                    a_t[here, :], right, preferred_element_type=f32
                ).astype(bf16)

    by_core(core_ref, body, first, second)


def grad_blocks(b, g_ref, outs, pair, transposed):
    cols = slice(pair * 256, (pair + 1) * 256)
    step = 256
    for r in range(0, half, step):
        left = jnp.concatenate([v[r : r + step, :] for v in b], axis=1)
        if transposed:
            part = lax.dot_general(
                left, g_ref[cols, :], (((1,), (1,)), ((), ())), preferred_element_type=f32
            )
        else:
            part = jnp.dot(left, g_ref[:, cols], preferred_element_type=f32)
        part = part.astype(bf16)
        outs[0][r : r + step, :] = part[:, :lanes]
        outs[1][r : r + step, :] = part[:, lanes:]


def all_grads(core_ref, first, second, g_ref, outs, pairs):
    def body(a, b):
        for n, pair in enumerate(pairs):
            both = outs[4 * n : 4 * n + 2], outs[4 * n + 2 : 4 * n + 4]
            of_a, of_b = both if a is first else both[::-1]
            grad_blocks(b, g_ref, of_a, pair, True)
            grad_blocks(a, g_ref, of_b, pair, False)

    by_core(core_ref, body, first, second)


def first_kernel(batch, core_ref, *refs):
    first_view, second_view = refs[:8], refs[8:16]
    mine, recv, diag_mine, diag_recv = refs[16:20]
    outs = refs[20:24]
    g_ref, loss_ref, diag_ref = refs[24:]
    size = mine.shape[0]
    diag = (diag_mine[...] + diag_recv[...]) / batch
    diag_ref[...] = diag
    missing = 1.0 - diag
    first = lax.broadcasted_iota(jnp.int32, (8, lanes), 0) == 0
    total = jnp.where(first, missing * missing, 0.0)
    step = 128
    for r in range(0, size, step):
        corr = (mine[r : r + step, :].astype(f32) + recv[r : r + step, :].astype(f32)) / batch
        if r == 0:
            ids = lax.broadcasted_iota(jnp.int32, (step, size), 0)
            corr = jnp.where(ids == lax.broadcasted_iota(jnp.int32, (step, size), 1), 0.0, corr)
        g_ref[r : r + step, :] = (2.0 * off_weight * corr).astype(bf16)
        square = jnp.sum((off_weight * corr * corr).reshape(step // 8, 8, size), axis=0)
        total = total + sum(square[:, c : c + lanes] for c in range(0, size, lanes))
    total = jnp.sum(total, axis=0, keepdims=True)
    high = total.astype(bf16)
    total = total - high.astype(f32)
    mid = total.astype(bf16)
    low = (total - mid.astype(f32)).astype(bf16)
    top = jnp.concatenate([high, mid, low, jnp.zeros((loss_rows - 3, lanes), bf16)], axis=0)
    loss_ref[...] = jnp.concatenate([top, jnp.zeros((loss_rows, lanes), bf16)], axis=1)
    all_grads(core_ref, first_view, second_view, g_ref, outs, (3,))


def rest_kernel(core_ref, *refs):
    first, second, g_ref, outs = refs[:8], refs[8:16], refs[16], refs[17:]
    all_grads(core_ref, first, second, g_ref, outs, (2, 1, 0))


def add_kernel(count, *refs):
    outs = refs[len(refs) // (count + 1) * count :]
    for n, out in enumerate(outs):
        terms = refs[count * n : count * n + count]
        out[...] = sum(t[...].astype(f32) for t in terms).astype(bf16)


def sums_kernel(x_ref, mine_ref, other_ref, diag_ref, *refs):
    parts_1, parts_2 = refs[:4], refs[4:8]
    full_ref, sums_ref = refs[8:]
    rows = x_ref.shape[0]
    mean, rstd = merge_stats(mine_ref[...], other_ref[...], rows)
    norm = (x_ref[...].astype(f32) - mean) * rstd
    rounded = norm.astype(bf16).astype(f32)
    coef = -2.0 * (1.0 - diag_ref[0:1, :])
    first = sum(p[...].astype(f32) for p in parts_1) + coef * rounded[:, lanes:]
    second = sum(p[...].astype(f32) for p in parts_2) + coef * rounded[:, :lanes]
    full = jnp.concatenate([first, second], axis=1)
    full_ref[...] = full
    s1 = jnp.sum(full, axis=0, keepdims=True)
    s2 = jnp.sum(full * norm, axis=0, keepdims=True)
    sums_ref[...] = jnp.concatenate([s1, s2, jnp.zeros((6, 2 * lanes), f32)], axis=0)


def final_kernel(x_ref, mine_ref, other_ref, full_ref, s_mine, s_other, out_ref):
    rows = x_ref.shape[0]
    mean, rstd = merge_stats(mine_ref[...], other_ref[...], rows)
    norm = (x_ref[...].astype(f32) - mean) * rstd
    other = s_other[...]
    other = jnp.concatenate([other[:, lanes:], other[:, :lanes]], axis=1)
    sums = (s_mine[...] + other) / (2 * rows)
    out_ref[...] = (rstd * (full_ref[...] - sums[0:1] - norm * sums[1:2])).astype(bf16)


def gather(own, role):
    side, left, right = gate(across(own, role), line(own, role, 1), line(own, role, -1))
    side_left, side_right = line(side, role, 1), across(right, role)
    opposite = line(right, role, -1)
    if role == 0:
        last = line(side_left, role, 1)
    else:
        last = line(side_right, role, -1)
    return [own, side, left, right, side_left, side_right, opposite, last]


def on_device(view_a, view_b):
    rows_dev, features = view_a.shape
    groups = features // lanes
    rows = rows_dev * groups
    batch = 2 * rows
    block = shape((rows, lanes), bf16)
    core = lax.axis_index("c").astype(jnp.int32)
    core_0 = core == 0

    def split(view):
        return view.reshape(rows_dev, groups, lanes).transpose(1, 0, 2)

    a, b = split(view_a), split(view_b)
    both = jnp.concatenate([jnp.where(core_0, a, b), jnp.where(core_0, b, a)], axis=2)
    x = lax.all_to_all(both, chips, 0, 0, tiled=True).reshape(rows, 2 * lanes)
    mine = call(stats_kernel, shape((8, 2 * lanes), f32), x)
    other = swap(mine)
    own_1, own_2, diag_mine = call(
        norm_kernel, (block, block, shape((8, lanes), f32)), x, mine, other
    )
    diag_other = swap(diag_mine)
    views = [*gather(own_1, 0), *gather(own_2, 1)]
    size = 8 * lanes
    work = 2 * rows * size * size
    place = core.reshape(1)
    corr_mine = call(
        corr_kernel,
        shape((size, size), bf16),
        place,
        *views,
        scratch=[pltpu.VMEM((size, rows), bf16)],
        flops=work,
        scalar=True,
    )
    corr_other = swap(corr_mine)
    *far, g, loss, diag = call(
        functools.partial(first_kernel, batch),
        (block,) * 4
        + (
            shape((size, size), bf16),
            shape((loss_rows, 2 * lanes), bf16),
            shape((8, lanes), f32),
        ),
        place,
        *views,
        corr_mine,
        corr_other,
        diag_mine,
        diag_other,
        flops=work // 2,
        scalar=True,
    )
    last_in = line(far[1], 0, -1), line(far[3], 1, 1)
    far_in = line(far[0], 0, 1), line(far[2], 1, 1)
    rest = call(
        rest_kernel, (block,) * 12, place, *views, g, flops=work * 3 // 2, scalar=True
    )

    def add(count, *terms):
        n = len(terms) // count
        return call(functools.partial(add_kernel, count), (block,) * n, *terms)

    side_left, side_right = rest[0:4:2], rest[1:4:2]
    left, right, own, side = rest[4:8:2], rest[5:8:2], rest[8:12:2], rest[9:12:2]
    sum_1, sum_2 = add(2, side_left[0], last_in[0], side_right[1], last_in[1])
    side_left, side_right = (sum_1, side_left[1]), (side_right[0], sum_2)
    side_in = [line(v, n, -1) for n, v in enumerate(side_left)]
    right_in = [across(v, n) for n, v in enumerate(side_right)]
    parts = []
    for n in range(2):
        (right_sum,) = add(3, right[n], right_in[n], far_in[n])
        (side_sum,) = add(2, side[n], side_in[n])
        parts += [own[n], line(left[n], n, -1), line(right_sum, n, 1), across(side_sum, n)]
    full, s_mine = call(
        sums_kernel,
        (shape((rows, 2 * lanes), f32), shape((8, 2 * lanes), f32)),
        x,
        mine,
        other,
        diag,
        *parts,
    )
    s_other = swap(s_mine)
    grads = call(
        final_kernel, shape((rows, 2 * lanes), bf16), x, mine, other, full, s_mine, s_other
    ).reshape(groups, rows_dev, 2 * lanes)
    loss = jnp.broadcast_to(loss[None], (groups,) + loss.shape)
    back = lax.all_to_all(jnp.concatenate([grads, loss], axis=1), chips, 0, 0, tiled=True)
    total = jnp.sum(back[:, rows_dev : rows_dev + 3, :lanes].astype(f32))
    back = back[:, :rows_dev, :].transpose(1, 0, 2)
    first, second = back[:, :, :lanes], back[:, :, lanes:]
    grad_a = jnp.where(core_0, first, second).reshape(rows_dev, features)
    grad_b = jnp.where(core_0, second, first).reshape(rows_dev, features)
    return (total / features, grad_a, grad_b)


def solution(mesh):
    split = Mesh(mesh.devices.reshape(sizes), axes)
    return jax.shard_map(
        on_device,
        mesh=split,
        in_specs=(P(axes, None), P(axes, None)),
        out_specs=(P(), P(axes, None), P(axes, None)),
        check_vma=False,
    )
```

```python
import functools

import jax
import jax.numpy as jnp
from jax import lax
from jax.experimental import pallas as pl
from jax.experimental.pallas import tpu as pltpu
from jax.sharding import Mesh, PartitionSpec as P

off_weight = 0.0051
norm_eps = 1e-05
bf16 = jnp.bfloat16
f32 = jnp.float32
axes = ("z", "x", "y", "c")
chips = ("z", "x", "y")
sizes = (4, 4, 4, 2)
lanes = 128
vmem_limit = 24 * 2**20
half = 2048
loss_rows = 8


def call(kernel, out_shape, *args, scratch=(), flops=0, scalar=False):
    one = isinstance(out_shape, jax.ShapeDtypeStruct)
    outs = [out_shape] if one else list(out_shape)
    vmem = pl.BlockSpec(memory_space=pltpu.VMEM)
    specs = [vmem] * len(args)
    if scalar:
        specs[0] = pl.BlockSpec(memory_space=pltpu.SMEM)
    traffic = sum(a.size * a.dtype.itemsize for a in list(args) + outs)
    return pl.pallas_call(
        kernel,
        out_shape=out_shape,
        in_specs=specs,
        out_specs=vmem if one else [vmem] * len(outs),
        scratch_shapes=list(scratch),
        compiler_params=pltpu.CompilerParams(vmem_limit_bytes=vmem_limit),
        cost_estimate=pl.CostEstimate(flops=flops, bytes_accessed=traffic, transcendentals=0),
    )(*args)


def shape(dims, dtype):
    return jax.ShapeDtypeStruct(dims, dtype)


def device(z, x, y, c):
    return ((z * 4 + x) * 4 + y) * 2 + c


def moved(target):
    places = [(z, x, y, c) for z in range(4) for x in range(4) for y in range(4) for c in range(2)]
    return [(device(*p), device(*target(*p))) for p in places]


def line(x, role, step):
    def target(z, x, y, c):
        return (z, x, (y + step) % 4, c) if c == role else ((z + step) % 4, x, y, c)

    return lax.ppermute(x, axes, moved(target))


def across(x, role):
    def target(z, x, y, c):
        return (z, x ^ 1 if c == role else 3 - x, y, c)

    return lax.ppermute(x, axes, moved(target))


def swap(x):
    return lax.ppermute(x, axes, moved(lambda z, x, y, c: (z, x, y, 1 - c)))


def gate_kernel(n, *refs):
    for x, out in zip(refs[:n], refs[-n:]):
        out[...] = x[...]


def gate(*xs, others=()):
    outs = [shape(x.shape, x.dtype) for x in xs]
    return call(functools.partial(gate_kernel, len(xs)), outs, *xs, *others)


def stats_kernel(x_ref, out_ref):
    x = x_ref[...].astype(f32)
    mean = jnp.mean(x, axis=0, keepdims=True)
    centred = x - mean
    m2 = jnp.sum(centred * centred, axis=0, keepdims=True)
    width = x.shape[1]
    out_ref[...] = jnp.concatenate([mean, m2, jnp.zeros((6, width), f32)], axis=0)


def merge_stats(mine, other, rows):
    other = jnp.concatenate([other[:, lanes:], other[:, :lanes]], axis=1)
    delta = other[0:1] - mine[0:1]
    mean = 0.5 * (mine[0:1] + other[0:1])
    var = (mine[1:2] + other[1:2]) / (2 * rows) + 0.25 * delta * delta
    return mean, lax.rsqrt(var + norm_eps)


def norm_kernel(x_ref, mine_ref, other_ref, a_ref, b_ref, diag_ref):
    rows = x_ref.shape[0]
    mean, rstd = merge_stats(mine_ref[...], other_ref[...], rows)
    norm = ((x_ref[...].astype(f32) - mean) * rstd).astype(bf16)
    a = norm[:, :lanes]
    b = norm[:, lanes:]
    a_ref[...] = a
    b_ref[...] = b
    diag = jnp.sum(a.astype(f32) * b.astype(f32), axis=0, keepdims=True)
    diag_ref[...] = jnp.broadcast_to(diag, diag_ref.shape)


def by_core(core_ref, body, first, second):
    @pl.when(core_ref[0] == 0)
    def _():
        body(first, second)

    @pl.when(core_ref[0] != 0)
    def _():
        body(second, first)


def corr_kernel(core_ref, *refs):
    first, second, out_ref, a_t = refs[:7], refs[7:14], refs[14], refs[15]

    def body(a, b):
        for i in range(7):
            a_t[i * lanes : (i + 1) * lanes, :] = a[i][...].T
        for q in range(0, 7, 2):
            right = jnp.concatenate([v[...] for v in b[q : q + 2]], axis=1)
            cols = slice(q * lanes, min(q + 2, 7) * lanes)
            for p in range(0, 7, 2):
                here = slice(p * lanes, min(p + 2, 7) * lanes)
                out_ref[here, cols] = jnp.dot(
                    a_t[here, :], right, preferred_element_type=f32
                ).astype(bf16)

    by_core(core_ref, body, first, second)


def corr_last_kernel(core_ref, *refs):
    first, second, out_ref = refs[:8], refs[8:16], refs[16]

    def body(a, b):
        a_t = a[7][...].T
        b_t = b[7][...].T
        for q in range(0, 8, 2):
            right = jnp.concatenate([b[q][...], b[q + 1][...]], axis=1)
            part = jnp.dot(a_t, right, preferred_element_type=f32).astype(bf16)
            out_ref[q * lanes : (q + 1) * lanes, :] = part[:, :lanes]
            out_ref[(q + 1) * lanes : (q + 2) * lanes, :] = part[:, lanes:]
        for p in range(0, 8, 2):
            right = jnp.concatenate([a[p][...], a[p + 1][...]], axis=1)
            part = jnp.dot(b_t, right, preferred_element_type=f32)
            for n in range(p, min(p + 2, 7)):
                block = part[:, (n - p) * lanes : (n - p + 1) * lanes].T
                out_ref[(8 + n) * lanes : (9 + n) * lanes, :] = block.astype(bf16)

    by_core(core_ref, body, first, second)


def main_g_kernel(batch, mine, recv, diag_mine, diag_recv, g_ref, loss_ref, diag_ref):
    size = mine.shape[0]
    diag = (diag_mine[...] + diag_recv[...]) * (1.0 / batch)
    diag_ref[...] = diag
    missing = 1.0 - diag
    first = lax.broadcasted_iota(jnp.int32, (8, lanes), 0) == 0
    total = jnp.zeros((8, lanes), f32)
    for r in range(0, size, lanes):
        both = mine[r : r + lanes, :].astype(f32) + recv[r : r + lanes, :].astype(f32)
        if r == 0:
            ids = lax.broadcasted_iota(jnp.int32, (lanes, size), 0)
            same = ids == lax.broadcasted_iota(jnp.int32, (lanes, size), 1)
            both = jnp.where(same, 0.0, both)
        g_ref[r : r + lanes, :] = (both * (2.0 * off_weight / batch)).astype(bf16)
        total = total + squares(both)
    total = total * (off_weight / (batch * batch))
    loss_ref[...] = total + jnp.where(first, missing * missing, 0.0)


def squares(x):
    square = jnp.sum((x * x).reshape(x.shape[0] // 8, 8, x.shape[1]), axis=0)
    return sum(square[:, c : c + lanes] for c in range(0, x.shape[1], lanes))


def grad_blocks(b, g_ref, outs, pair, transposed):
    cols = slice(pair * 256, (pair + 1) * 256)
    step = 256
    for r in range(0, half, step):
        left = jnp.concatenate([v[r : r + step, :] for v in b], axis=1)
        if transposed:
            part = lax.dot_general(
                left, g_ref[cols, :], (((1,), (1,)), ((), ())), preferred_element_type=f32
            )
        else:
            part = jnp.dot(left, g_ref[:, cols], preferred_element_type=f32)
        part = part.astype(bf16)
        outs[0][r : r + step, :] = part[:, :lanes]
        outs[1][r : r + step, :] = part[:, lanes:]


def all_grads(core_ref, first, second, g_ref, outs, pairs):
    def body(a, b):
        for n, pair in enumerate(pairs):
            both = outs[4 * n : 4 * n + 2], outs[4 * n + 2 : 4 * n + 4]
            of_a, of_b = both if a is first else both[::-1]
            grad_blocks(b, g_ref, of_a, pair, True)
            grad_blocks(a, g_ref, of_b, pair, False)

    by_core(core_ref, body, first, second)


def first_kernel(batch, core_ref, *refs):
    first_view, second_view = refs[:8], refs[8:16]
    main, loss_main, mine, recv = refs[16:20]
    outs = refs[20:24]
    g_ref, loss_ref = refs[24:]
    size = 7 * lanes
    g_ref[:size, :size] = main[...]
    total = jnp.zeros((8, lanes), f32)
    for n in range(15):
        rows = slice(n * lanes, (n + 1) * lanes)
        both = mine[rows, :].astype(f32) + recv[rows, :].astype(f32)
        total = total + squares(both)
        both = (both * (2.0 * off_weight / batch)).astype(bf16)
        if n < 8:
            g_ref[size:, rows] = both
        else:
            g_ref[(n - 8) * lanes : (n - 7) * lanes, size:] = both
    total = loss_main[...] + total * (off_weight / (batch * batch))
    total = jnp.sum(total, axis=0, keepdims=True)
    high = total.astype(bf16)
    total = total - high.astype(f32)
    mid = total.astype(bf16)
    low = (total - mid.astype(f32)).astype(bf16)
    top = jnp.concatenate([high, mid, low, jnp.zeros((loss_rows - 3, lanes), bf16)], axis=0)
    loss_ref[...] = jnp.concatenate([top, jnp.zeros((loss_rows, lanes), bf16)], axis=1)
    all_grads(core_ref, first_view, second_view, g_ref, outs, (3,))


def rest_kernel(core_ref, *refs):
    first, second, g_ref, outs = refs[:8], refs[8:16], refs[16], refs[17:]
    all_grads(core_ref, first, second, g_ref, outs, (2, 1, 0))


def add_kernel(count, sums, *refs):
    for n, out in enumerate(refs[-sums:]):
        terms = refs[count * n : count * n + count]
        out[...] = sum(t[...].astype(f32) for t in terms).astype(bf16)


def sums_kernel(x_ref, mine_ref, other_ref, diag_ref, *refs):
    parts_1, parts_2 = refs[:4], refs[4:8]
    full_ref, sums_ref = refs[8:]
    rows = x_ref.shape[0]
    mean, rstd = merge_stats(mine_ref[...], other_ref[...], rows)
    norm = (x_ref[...].astype(f32) - mean) * rstd
    rounded = norm.astype(bf16).astype(f32)
    coef = -2.0 * (1.0 - diag_ref[0:1, :])
    first = sum(p[...].astype(f32) for p in parts_1) + coef * rounded[:, lanes:]
    second = sum(p[...].astype(f32) for p in parts_2) + coef * rounded[:, :lanes]
    full = jnp.concatenate([first, second], axis=1)
    full_ref[...] = full
    s1 = jnp.sum(full, axis=0, keepdims=True)
    s2 = jnp.sum(full * norm, axis=0, keepdims=True)
    sums_ref[...] = jnp.concatenate([s1, s2, jnp.zeros((6, 2 * lanes), f32)], axis=0)


def final_kernel(x_ref, mine_ref, other_ref, full_ref, s_mine, s_other, out_ref):
    rows = x_ref.shape[0]
    mean, rstd = merge_stats(mine_ref[...], other_ref[...], rows)
    norm = (x_ref[...].astype(f32) - mean) * rstd
    other = s_other[...]
    other = jnp.concatenate([other[:, lanes:], other[:, :lanes]], axis=1)
    sums = (s_mine[...] + other) / (2 * rows)
    out_ref[...] = (rstd * (full_ref[...] - sums[0:1] - norm * sums[1:2])).astype(bf16)


def gather(own, role):
    side, left, right = across(own, role), line(own, role, 1), line(own, role, -1)
    if role == 0:
        side, left, right = gate(side, left, right)
        side_left, side_right = line(side, role, 1), across(right, role)
        opposite = line(right, role, -1)
        last = line(side_left, role, 1)
    else:
        left, right = gate(left, right)
        side_right = across(right, role)
        last = line(side_right, role, -1)
        side, far = gate(side, right)
        side_left, opposite = line(side, role, 1), line(far, role, -1)
    return [own, side, left, right, side_left, side_right, opposite, last]


def on_device(view_a, view_b):
    rows_dev, features = view_a.shape
    groups = features // lanes
    rows = rows_dev * groups
    batch = 2 * rows
    block = shape((rows, lanes), bf16)
    core = lax.axis_index("c").astype(jnp.int32)
    core_0 = core == 0

    def split(view):
        return view.reshape(rows_dev, groups, lanes).transpose(1, 0, 2)

    a, b = split(view_a), split(view_b)
    both = jnp.concatenate([jnp.where(core_0, a, b), jnp.where(core_0, b, a)], axis=2)
    x = lax.all_to_all(both, chips, 0, 0, tiled=True).reshape(rows, 2 * lanes)
    mine = call(stats_kernel, shape((8, 2 * lanes), f32), x)
    other = swap(mine)
    own_1, own_2, diag_mine = call(
        norm_kernel, (block, block, shape((8, lanes), f32)), x, mine, other
    )
    diag_other = swap(diag_mine)
    views = [*gather(own_1, 0), *gather(own_2, 1)]
    size = 8 * lanes
    work = 2 * rows * size * size
    place = core.reshape(1)
    main = 7 * lanes
    corr_mine = call(
        corr_kernel,
        shape((main, main), bf16),
        place,
        *views[:7],
        *views[8:15],
        scratch=[pltpu.VMEM((main, rows), bf16)],
        flops=work * 3 // 4,
        scalar=True,
    )
    g_main, loss_main, diag = call(
        functools.partial(main_g_kernel, batch),
        (shape((main, main), bf16), shape((8, lanes), f32), shape((8, lanes), f32)),
        corr_mine,
        swap(*gate(corr_mine, others=(views[7], views[15]))),
        diag_mine,
        diag_other,
    )
    last_mine = call(
        corr_last_kernel,
        shape((15 * lanes, lanes), bf16),
        place,
        *views,
        flops=work // 4,
        scalar=True,
    )
    *far, g, loss = call(
        functools.partial(first_kernel, batch),
        (block,) * 4 + (shape((size, size), bf16), shape((loss_rows, 2 * lanes), bf16)),
        place,
        *views,
        g_main,
        loss_main,
        last_mine,
        swap(last_mine),
        flops=work // 2,
        scalar=True,
    )
    last_in = line(far[1], 0, -1), line(far[3], 1, 1)
    far_in = line(far[0], 0, 1), line(far[2], 1, 1)
    rest = call(
        rest_kernel, (block,) * 12, place, *views, g, flops=work * 3 // 2, scalar=True
    )

    def add(count, *terms, others=()):
        n = len(terms) // count
        return call(functools.partial(add_kernel, count, n), (block,) * n, *terms, *others)

    side_left, side_right = rest[0:4:2], rest[1:4:2]
    left, right, own, side = rest[4:8:2], rest[5:8:2], rest[8:12:2], rest[9:12:2]
    (sum_1,) = add(2, side_left[0], last_in[0])
    (sum_2,) = add(2, side_right[1], last_in[1], others=far_in[:1])
    side_left, side_right = (sum_1, side_left[1]), (side_right[0], sum_2)
    side_in = [line(v, n, -1) for n, v in enumerate(side_left)]
    right_in = [across(v, n) for n, v in enumerate(side_right)]
    parts = []
    for n in range(2):
        (right_sum,) = add(3, right[n], right_in[n], far_in[n])
        (side_sum,) = add(2, side[n], side_in[n])
        parts += [own[n], line(left[n], n, -1), line(right_sum, n, 1), across(side_sum, n)]
    full, s_mine = call(
        sums_kernel,
        (shape((rows, 2 * lanes), f32), shape((8, 2 * lanes), f32)),
        x,
        mine,
        other,
        diag,
        *parts,
    )
    s_other = swap(s_mine)
    grads = call(
        final_kernel, shape((rows, 2 * lanes), bf16), x, mine, other, full, s_mine, s_other
    ).reshape(groups, rows_dev, 2 * lanes)
    loss = jnp.broadcast_to(loss[None], (groups,) + loss.shape)
    back = lax.all_to_all(jnp.concatenate([grads, loss], axis=1), chips, 0, 0, tiled=True)
    total = jnp.sum(back[:, rows_dev : rows_dev + 3, :lanes].astype(f32))
    back = back[:, :rows_dev, :].transpose(1, 0, 2)
    first, second = back[:, :, :lanes], back[:, :, lanes:]
    grad_a = jnp.where(core_0, first, second).reshape(rows_dev, features)
    grad_b = jnp.where(core_0, second, first).reshape(rows_dev, features)
    return (total / features, grad_a, grad_b)


def solution(mesh):
    split = Mesh(mesh.devices.reshape(sizes), axes)
    return jax.shard_map(
        on_device,
        mesh=split,
        in_specs=(P(axes, None), P(axes, None)),
        out_specs=(P(), P(axes, None), P(axes, None)),
        check_vma=False,
    )
```

```python
import functools

import jax
import jax.numpy as jnp
from jax import lax
from jax.experimental import pallas as pl
from jax.experimental.pallas import tpu as pltpu
from jax.sharding import Mesh, PartitionSpec as P

off_weight = 0.0051
norm_eps = 1e-05
bf16 = jnp.bfloat16
f32 = jnp.float32
axes = ("z", "x", "y", "c")
chips = ("z", "x", "y")
sizes = (4, 4, 4, 2)
lanes = 128
vmem_limit = 24 * 2**20
half = 2048
loss_rows = 8


def call(kernel, out_shape, *args, scratch=(), flops=0, scalar=False, last_scalar=False):
    one = isinstance(out_shape, jax.ShapeDtypeStruct)
    outs = [out_shape] if one else list(out_shape)
    vmem = pl.BlockSpec(memory_space=pltpu.VMEM)
    specs = [vmem] * len(args)
    if scalar:
        specs[0] = pl.BlockSpec(memory_space=pltpu.SMEM)
    out_specs = [vmem] * len(outs)
    if last_scalar:
        out_specs[-1] = pl.BlockSpec(memory_space=pltpu.SMEM)
    traffic = sum(a.size * a.dtype.itemsize for a in list(args) + outs)
    return pl.pallas_call(
        kernel,
        out_shape=out_shape,
        in_specs=specs,
        out_specs=vmem if one else out_specs,
        scratch_shapes=list(scratch),
        compiler_params=pltpu.CompilerParams(vmem_limit_bytes=vmem_limit),
        cost_estimate=pl.CostEstimate(flops=flops, bytes_accessed=traffic, transcendentals=0),
    )(*args)


def shape(dims, dtype):
    return jax.ShapeDtypeStruct(dims, dtype)


def device(z, x, y, c):
    return ((z * 4 + x) * 4 + y) * 2 + c


def moved(target):
    places = [(z, x, y, c) for z in range(4) for x in range(4) for y in range(4) for c in range(2)]
    return [(device(*p), device(*target(*p))) for p in places]


def line(x, role, step):
    def target(z, x, y, c):
        return (z, x, (y + step) % 4, c) if c == role else ((z + step) % 4, x, y, c)

    return lax.ppermute(x, axes, moved(target))


def across(x, role):
    def target(z, x, y, c):
        return (z, x ^ 1 if c == role else 3 - x, y, c)

    return lax.ppermute(x, axes, moved(target))


def swap(x):
    return lax.ppermute(x, axes, moved(lambda z, x, y, c: (z, x, y, 1 - c)))


def gate_kernel(n, *refs):
    for x, out in zip(refs[:n], refs[-n:]):
        out[...] = x[...]


def gate(*xs, others=()):
    outs = [shape(x.shape, x.dtype) for x in xs]
    return call(functools.partial(gate_kernel, len(xs)), outs, *xs, *others)


def stats_kernel(x_ref, out_ref):
    x = x_ref[...].astype(f32)
    mean = jnp.mean(x, axis=0, keepdims=True)
    centred = x - mean
    m2 = jnp.sum(centred * centred, axis=0, keepdims=True)
    width = x.shape[1]
    out_ref[...] = jnp.concatenate([mean, m2, jnp.zeros((6, width), f32)], axis=0)


def merge_stats(mine, other, rows):
    other = jnp.concatenate([other[:, lanes:], other[:, :lanes]], axis=1)
    delta = other[0:1] - mine[0:1]
    mean = 0.5 * (mine[0:1] + other[0:1])
    var = (mine[1:2] + other[1:2]) / (2 * rows) + 0.25 * delta * delta
    return mean, lax.rsqrt(var + norm_eps)


def norm_kernel(x_ref, mine_ref, other_ref, a_ref, b_ref, diag_ref):
    rows = x_ref.shape[0]
    mean, rstd = merge_stats(mine_ref[...], other_ref[...], rows)
    norm = ((x_ref[...].astype(f32) - mean) * rstd).astype(bf16)
    a = norm[:, :lanes]
    b = norm[:, lanes:]
    a_ref[...] = a
    b_ref[...] = b
    diag = jnp.sum(a.astype(f32) * b.astype(f32), axis=0, keepdims=True)
    diag_ref[...] = jnp.broadcast_to(diag, diag_ref.shape)


def by_core(core_ref, body, first, second):
    @pl.when(core_ref[0] == 0)
    def _():
        body(first, second)

    @pl.when(core_ref[0] != 0)
    def _():
        body(second, first)


def corr_kernel(core_ref, *refs):
    first, second, out_ref, a_t = refs[:7], refs[7:14], refs[14], refs[15]

    def body(a, b):
        for i in range(7):
            a_t[i * lanes : (i + 1) * lanes, :] = a[i][...].T
        for q in range(0, 7, 2):
            right = jnp.concatenate([v[...] for v in b[q : q + 2]], axis=1)
            cols = slice(q * lanes, min(q + 2, 7) * lanes)
            for p in range(0, 7, 2):
                here = slice(p * lanes, min(p + 2, 7) * lanes)
                out_ref[here, cols] = jnp.dot(
                    a_t[here, :], right, preferred_element_type=f32
                ).astype(bf16)

    by_core(core_ref, body, first, second)


def corr_last_kernel(core_ref, *refs):
    first, second, out_ref = refs[:8], refs[8:16], refs[16]

    def body(a, b):
        a_t = a[7][...].T
        b_t = b[7][...].T
        for q in range(0, 8, 2):
            right = jnp.concatenate([b[q][...], b[q + 1][...]], axis=1)
            part = jnp.dot(a_t, right, preferred_element_type=f32).astype(bf16)
            out_ref[q * lanes : (q + 1) * lanes, :] = part[:, :lanes]
            out_ref[(q + 1) * lanes : (q + 2) * lanes, :] = part[:, lanes:]
        for p in range(0, 8, 2):
            right = jnp.concatenate([a[p][...], a[p + 1][...]], axis=1)
            part = jnp.dot(b_t, right, preferred_element_type=f32)
            for n in range(p, min(p + 2, 7)):
                block = part[:, (n - p) * lanes : (n - p + 1) * lanes].T
                out_ref[(8 + n) * lanes : (9 + n) * lanes, :] = block.astype(bf16)

    by_core(core_ref, body, first, second)


def main_g_kernel(batch, mine, recv, diag_mine, diag_recv, g_ref, loss_ref, diag_ref):
    size = mine.shape[0]
    diag = (diag_mine[...] + diag_recv[...]) * (1.0 / batch)
    diag_ref[...] = diag
    missing = 1.0 - diag
    first = lax.broadcasted_iota(jnp.int32, (8, lanes), 0) == 0
    total = jnp.zeros((8, lanes), f32)
    for r in range(0, size, lanes):
        both = mine[r : r + lanes, :].astype(f32) + recv[r : r + lanes, :].astype(f32)
        if r == 0:
            ids = lax.broadcasted_iota(jnp.int32, (lanes, size), 0)
            same = ids == lax.broadcasted_iota(jnp.int32, (lanes, size), 1)
            both = jnp.where(same, 0.0, both)
        g_ref[r : r + lanes, :] = (both * (2.0 * off_weight / batch)).astype(bf16)
        total = total + squares(both)
    total = total * (off_weight / (batch * batch))
    loss_ref[...] = total + jnp.where(first, missing * missing, 0.0)


def squares(x):
    square = jnp.sum((x * x).reshape(x.shape[0] // 8, 8, x.shape[1]), axis=0)
    return sum(square[:, c : c + lanes] for c in range(0, x.shape[1], lanes))


def grad_blocks(b, g_ref, outs, pair, transposed):
    cols = slice(pair * 256, (pair + 1) * 256)
    step = 256
    for r in range(0, half, step):
        left = jnp.concatenate([v[r : r + step, :] for v in b], axis=1)
        if transposed:
            part = lax.dot_general(
                left, g_ref[cols, :], (((1,), (1,)), ((), ())), preferred_element_type=f32
            )
        else:
            part = jnp.dot(left, g_ref[:, cols], preferred_element_type=f32)
        part = part.astype(bf16)
        outs[0][r : r + step, :] = part[:, :lanes]
        outs[1][r : r + step, :] = part[:, lanes:]


def all_grads(core_ref, first, second, g_ref, outs, pairs):
    def body(a, b):
        for n, pair in enumerate(pairs):
            both = outs[4 * n : 4 * n + 2], outs[4 * n + 2 : 4 * n + 4]
            of_a, of_b = both if a is first else both[::-1]
            grad_blocks(b, g_ref, of_a, pair, True)
            grad_blocks(a, g_ref, of_b, pair, False)

    by_core(core_ref, body, first, second)


def first_kernel(batch, core_ref, *refs):
    first_view, second_view = refs[:8], refs[8:16]
    main, loss_main, mine, recv = refs[16:20]
    outs = refs[20:24]
    g_ref, loss_ref = refs[24:]
    size = 7 * lanes
    g_ref[:size, :size] = main[...]
    total = jnp.zeros((8, lanes), f32)
    for n in range(15):
        rows = slice(n * lanes, (n + 1) * lanes)
        both = mine[rows, :].astype(f32) + recv[rows, :].astype(f32)
        total = total + squares(both)
        both = (both * (2.0 * off_weight / batch)).astype(bf16)
        if n < 8:
            g_ref[size:, rows] = both
        else:
            g_ref[(n - 8) * lanes : (n - 7) * lanes, size:] = both
    total = loss_main[...] + total * (off_weight / (batch * batch))
    total = jnp.sum(total, axis=0, keepdims=True)
    high = total.astype(bf16)
    total = total - high.astype(f32)
    mid = total.astype(bf16)
    low = (total - mid.astype(f32)).astype(bf16)
    loss_ref[...] = jnp.concatenate(
        [high, mid, low, jnp.zeros((loss_rows - 3, lanes), bf16)], axis=0
    )
    all_grads(core_ref, first_view, second_view, g_ref, outs, (3,))


def rest_kernel(core_ref, *refs):
    first, second, g_ref, outs = refs[:8], refs[8:16], refs[16], refs[17:]
    all_grads(core_ref, first, second, g_ref, outs, (2, 1, 0))


def add_kernel(count, sums, *refs):
    for n, out in enumerate(refs[-sums:]):
        terms = refs[count * n : count * n + count]
        out[...] = sum(t[...].astype(f32) for t in terms).astype(bf16)


def sums_kernel(x_ref, mine_ref, other_ref, diag_ref, *refs):
    parts_1, parts_2 = refs[:4], refs[4:8]
    full_ref, sums_ref = refs[8:]
    rows = x_ref.shape[0]
    mean, rstd = merge_stats(mine_ref[...], other_ref[...], rows)
    norm = (x_ref[...].astype(f32) - mean) * rstd
    rounded = norm.astype(bf16).astype(f32)
    coef = -2.0 * (1.0 - diag_ref[0:1, :])
    first = sum(p[...].astype(f32) for p in parts_1) + coef * rounded[:, lanes:]
    second = sum(p[...].astype(f32) for p in parts_2) + coef * rounded[:, :lanes]
    full = jnp.concatenate([first, second], axis=1)
    full_ref[...] = full
    s1 = jnp.sum(full, axis=0, keepdims=True)
    s2 = jnp.sum(full * norm, axis=0, keepdims=True)
    sums_ref[...] = jnp.concatenate([s1, s2, jnp.zeros((6, 2 * lanes), f32)], axis=0)


def final_kernel(x_ref, mine_ref, other_ref, full_ref, s_mine, s_other, loss_ref, out_ref):
    rows = x_ref.shape[0]
    groups = out_ref.shape[0]
    share = rows // groups
    mean, rstd = merge_stats(mine_ref[...], other_ref[...], rows)
    norm = (x_ref[...].astype(f32) - mean) * rstd
    other = s_other[...]
    other = jnp.concatenate([other[:, lanes:], other[:, :lanes]], axis=1)
    sums = (s_mine[...] + other) / (2 * rows)
    grad = (rstd * (full_ref[...] - sums[0:1] - norm * sums[1:2])).astype(bf16)
    grad = grad.reshape(groups, share, 2 * lanes)
    out_ref[:, :share, :] = grad[:, :, :lanes]
    out_ref[:, share : 2 * share, :] = grad[:, :, lanes:]
    loss = loss_ref[...][None]
    out_ref[:, 2 * share :, :] = jnp.broadcast_to(loss, (groups,) + loss_ref.shape)


def rows_kernel(core_ref, x_ref, a_ref, b_ref, loss_ref):
    share = a_ref.shape[0]

    def body(a, b):
        for g in range(x_ref.shape[0]):
            cols = slice(g * lanes, (g + 1) * lanes)
            a[:, cols] = x_ref[g, :share, :]
            b[:, cols] = x_ref[g, share : 2 * share, :]

    by_core(core_ref, body, a_ref, b_ref)
    loss = jnp.sum(x_ref[:, 2 * share :, :].astype(f32), axis=0)
    loss_ref[0, 0] = jnp.sum(loss) * (1.0 / a_ref.shape[1])


def gather(own, role):
    side, left, right = across(own, role), line(own, role, 1), line(own, role, -1)
    if role == 0:
        side, left, right = gate(side, left, right)
        side_left, side_right = line(side, role, 1), across(right, role)
        opposite = line(right, role, -1)
        last = line(side_left, role, 1)
    else:
        left, right = gate(left, right)
        side_right = across(right, role)
        last = line(side_right, role, -1)
        side, far = gate(side, right)
        side_left, opposite = line(side, role, 1), line(far, role, -1)
    return [own, side, left, right, side_left, side_right, opposite, last]


def on_device(view_a, view_b):
    rows_dev, features = view_a.shape
    groups = features // lanes
    rows = rows_dev * groups
    batch = 2 * rows
    block = shape((rows, lanes), bf16)
    core = lax.axis_index("c").astype(jnp.int32)
    core_0 = core == 0

    def split(view):
        return view.reshape(rows_dev, groups, lanes).transpose(1, 0, 2)

    a, b = split(view_a), split(view_b)
    both = jnp.concatenate([jnp.where(core_0, a, b), jnp.where(core_0, b, a)], axis=2)
    x = lax.all_to_all(both, chips, 0, 0, tiled=True).reshape(rows, 2 * lanes)
    mine = call(stats_kernel, shape((8, 2 * lanes), f32), x)
    other = swap(mine)
    own_1, own_2, diag_mine = call(
        norm_kernel, (block, block, shape((8, lanes), f32)), x, mine, other
    )
    diag_other = swap(diag_mine)
    views = [*gather(own_1, 0), *gather(own_2, 1)]
    size = 8 * lanes
    work = 2 * rows * size * size
    place = core.reshape(1)
    main = 7 * lanes
    corr_mine = call(
        corr_kernel,
        shape((main, main), bf16),
        place,
        *views[:7],
        *views[8:15],
        scratch=[pltpu.VMEM((main, rows), bf16)],
        flops=work * 3 // 4,
        scalar=True,
    )
    g_main, loss_main, diag = call(
        functools.partial(main_g_kernel, batch),
        (shape((main, main), bf16), shape((8, lanes), f32), shape((8, lanes), f32)),
        corr_mine,
        swap(*gate(corr_mine, others=(views[7], views[15]))),
        diag_mine,
        diag_other,
    )
    last_mine = call(
        corr_last_kernel,
        shape((15 * lanes, lanes), bf16),
        place,
        *views,
        flops=work // 4,
        scalar=True,
    )
    *far, g, loss = call(
        functools.partial(first_kernel, batch),
        (block,) * 4 + (shape((size, size), bf16), shape((loss_rows, lanes), bf16)),
        place,
        *views,
        g_main,
        loss_main,
        last_mine,
        swap(last_mine),
        flops=work // 2,
        scalar=True,
    )
    last_in = line(far[1], 0, -1), line(far[3], 1, 1)
    far_in = line(far[0], 0, 1), line(far[2], 1, 1)
    rest = call(
        rest_kernel, (block,) * 12, place, *views, g, flops=work * 3 // 2, scalar=True
    )

    def add(count, *terms, others=()):
        n = len(terms) // count
        return call(functools.partial(add_kernel, count, n), (block,) * n, *terms, *others)

    side_left, side_right = rest[0:4:2], rest[1:4:2]
    left, right, own, side = rest[4:8:2], rest[5:8:2], rest[8:12:2], rest[9:12:2]
    (sum_1,) = add(2, side_left[0], last_in[0])
    (sum_2,) = add(2, side_right[1], last_in[1], others=far_in[:1])
    side_left, side_right = (sum_1, side_left[1]), (side_right[0], sum_2)
    side_in = [line(v, n, -1) for n, v in enumerate(side_left)]
    right_in = [across(v, n) for n, v in enumerate(side_right)]
    parts = []
    for n in range(2):
        (right_sum,) = add(3, right[n], right_in[n], far_in[n])
        (side_sum,) = add(2, side[n], side_in[n])
        parts += [own[n], line(left[n], n, -1), line(right_sum, n, 1), across(side_sum, n)]
    full, s_mine = call(
        sums_kernel,
        (shape((rows, 2 * lanes), f32), shape((8, 2 * lanes), f32)),
        x,
        mine,
        other,
        diag,
        *parts,
    )
    s_other = swap(s_mine)
    grads = call(
        final_kernel,
        shape((groups, 2 * rows_dev + loss_rows, lanes), bf16),
        x,
        mine,
        other,
        full,
        s_mine,
        s_other,
        loss,
    )
    back = lax.all_to_all(grads, chips, 0, 0, tiled=True)
    grad_a, grad_b, total = call(
        rows_kernel,
        (*[shape((rows_dev, features), bf16)] * 2, shape((1, 1), f32)),
        place,
        back,
        scalar=True,
        last_scalar=True,
    )
    return (total.reshape(()), grad_a, grad_b)


def solution(mesh):
    split = Mesh(mesh.devices.reshape(sizes), axes)
    return jax.shard_map(
        on_device,
        mesh=split,
        in_specs=(P(axes, None), P(axes, None)),
        out_specs=(P(), P(axes, None), P(axes, None)),
        check_vma=False,
    )
```

```python
import functools

import jax
import jax.numpy as jnp
from jax import lax
from jax.experimental import pallas as pl
from jax.experimental.pallas import tpu as pltpu
from jax.sharding import Mesh, PartitionSpec as P

off_weight = 0.0051
norm_eps = 1e-05
bf16 = jnp.bfloat16
f32 = jnp.float32
axes = ("z", "x", "y", "c")
chips = ("z", "x", "y")
sizes = (4, 4, 4, 2)
lanes = 128
vmem_limit = 24 * 2**20
half = 2048
loss_rows = 16


def call(kernel, out_shape, *args, scratch=(), flops=0, scalar=False, last_scalar=False):
    one = isinstance(out_shape, jax.ShapeDtypeStruct)
    outs = [out_shape] if one else list(out_shape)
    vmem = pl.BlockSpec(memory_space=pltpu.VMEM)
    specs = [vmem] * len(args)
    if scalar:
        specs[0] = pl.BlockSpec(memory_space=pltpu.SMEM)
    out_specs = [vmem] * len(outs)
    if last_scalar:
        out_specs[-1] = pl.BlockSpec(memory_space=pltpu.SMEM)
    traffic = sum(a.size * a.dtype.itemsize for a in list(args) + outs)
    return pl.pallas_call(
        kernel,
        out_shape=out_shape,
        in_specs=specs,
        out_specs=vmem if one else out_specs,
        scratch_shapes=list(scratch),
        compiler_params=pltpu.CompilerParams(vmem_limit_bytes=vmem_limit),
        cost_estimate=pl.CostEstimate(flops=flops, bytes_accessed=traffic, transcendentals=0),
    )(*args)


def shape(dims, dtype):
    return jax.ShapeDtypeStruct(dims, dtype)


def device(z, x, y, c):
    return ((z * 4 + x) * 4 + y) * 2 + c


def moved(target):
    places = [(z, x, y, c) for z in range(4) for x in range(4) for y in range(4) for c in range(2)]
    return [(device(*p), device(*target(*p))) for p in places]


def line(x, role, step):
    def target(z, x, y, c):
        return (z, x, (y + step) % 4, c) if c == role else ((z + step) % 4, x, y, c)

    return lax.ppermute(x, axes, moved(target))


def across(x, role):
    def target(z, x, y, c):
        return (z, x ^ 1 if c == role else 3 - x, y, c)

    return lax.ppermute(x, axes, moved(target))


def swap(x):
    return lax.ppermute(x, axes, moved(lambda z, x, y, c: (z, x, y, 1 - c)))


def gate_kernel(n, *refs):
    for x, out in zip(refs[:n], refs[-n:]):
        out[...] = x[...]


def gate(*xs, others=()):
    outs = [shape(x.shape, x.dtype) for x in xs]
    return call(functools.partial(gate_kernel, len(xs)), outs, *xs, *others)


def stats_kernel(x_ref, out_ref):
    x = x_ref[...].astype(f32)
    mean = jnp.mean(x, axis=0, keepdims=True)
    centred = x - mean
    m2 = jnp.sum(centred * centred, axis=0, keepdims=True)
    width = x.shape[1]
    out_ref[...] = jnp.concatenate([mean, m2, jnp.zeros((6, width), f32)], axis=0)


def merge_stats(mine, other, rows):
    other = jnp.concatenate([other[:, lanes:], other[:, :lanes]], axis=1)
    delta = other[0:1] - mine[0:1]
    mean = 0.5 * (mine[0:1] + other[0:1])
    var = (mine[1:2] + other[1:2]) / (2 * rows) + 0.25 * delta * delta
    return mean, lax.rsqrt(var + norm_eps)


def norm_kernel(x_ref, mine_ref, other_ref, a_ref, b_ref, diag_ref):
    rows = x_ref.shape[0]
    mean, rstd = merge_stats(mine_ref[...], other_ref[...], rows)
    norm = ((x_ref[...].astype(f32) - mean) * rstd).astype(bf16)
    a = norm[:, :lanes]
    b = norm[:, lanes:]
    a_ref[...] = a
    b_ref[...] = b
    diag = jnp.sum(a.astype(f32) * b.astype(f32), axis=0, keepdims=True)
    diag_ref[...] = jnp.broadcast_to(diag, diag_ref.shape)


def by_core(core_ref, body, first, second):
    @pl.when(core_ref[0] == 0)
    def _():
        body(first, second)

    @pl.when(core_ref[0] != 0)
    def _():
        body(second, first)


def corr_kernel(core_ref, *refs):
    first, second, out_ref, a_t = refs[:7], refs[7:14], refs[14], refs[15]

    def body(a, b):
        for i in range(7):
            a_t[i * lanes : (i + 1) * lanes, :] = a[i][...].T
        for q in range(0, 7, 2):
            right = jnp.concatenate([v[...] for v in b[q : q + 2]], axis=1)
            cols = slice(q * lanes, min(q + 2, 7) * lanes)
            for p in range(0, 7, 2):
                here = slice(p * lanes, min(p + 2, 7) * lanes)
                out_ref[here, cols] = jnp.dot(
                    a_t[here, :], right, preferred_element_type=f32
                ).astype(bf16)

    by_core(core_ref, body, first, second)


def corr_last_kernel(core_ref, *refs):
    first, second, out_ref = refs[:8], refs[8:16], refs[16]

    def body(a, b):
        a_t = a[7][...].T
        b_t = b[7][...].T
        for q in range(0, 8, 2):
            right = jnp.concatenate([b[q][...], b[q + 1][...]], axis=1)
            part = jnp.dot(a_t, right, preferred_element_type=f32).astype(bf16)
            out_ref[q * lanes : (q + 1) * lanes, :] = part[:, :lanes]
            out_ref[(q + 1) * lanes : (q + 2) * lanes, :] = part[:, lanes:]
        for p in range(0, 8, 2):
            right = jnp.concatenate([a[p][...], a[p + 1][...]], axis=1)
            part = jnp.dot(b_t, right, preferred_element_type=f32)
            for n in range(p, min(p + 2, 7)):
                block = part[:, (n - p) * lanes : (n - p + 1) * lanes].T
                out_ref[(8 + n) * lanes : (9 + n) * lanes, :] = block.astype(bf16)

    by_core(core_ref, body, first, second)


def main_g_kernel(batch, mine, recv, diag_mine, diag_recv, g_ref, loss_ref, diag_ref):
    size = mine.shape[0]
    diag = (diag_mine[...] + diag_recv[...]) * (1.0 / batch)
    diag_ref[...] = diag
    missing = 1.0 - diag
    first = lax.broadcasted_iota(jnp.int32, (8, lanes), 0) == 0
    total = jnp.zeros((8, lanes), f32)
    for r in range(0, size, lanes):
        both = mine[r : r + lanes, :].astype(f32) + recv[r : r + lanes, :].astype(f32)
        if r == 0:
            ids = lax.broadcasted_iota(jnp.int32, (lanes, size), 0)
            same = ids == lax.broadcasted_iota(jnp.int32, (lanes, size), 1)
            both = jnp.where(same, 0.0, both)
        g_ref[r : r + lanes, :] = (both * (2.0 * off_weight / batch)).astype(bf16)
        total = total + squares(both)
    total = total * (off_weight / (batch * batch))
    loss_ref[...] = total + jnp.where(first, missing * missing, 0.0)


def squares(x):
    square = jnp.sum((x * x).reshape(x.shape[0] // 8, 8, x.shape[1]), axis=0)
    return sum(square[:, c : c + lanes] for c in range(0, x.shape[1], lanes))


def grad_blocks(b, g_ref, outs, pair, transposed):
    cols = slice(pair * 256, (pair + 1) * 256)
    step = 256
    for r in range(0, half, step):
        left = jnp.concatenate([v[r : r + step, :] for v in b], axis=1)
        if transposed:
            part = lax.dot_general(
                left, g_ref[cols, :], (((1,), (1,)), ((), ())), preferred_element_type=f32
            )
        else:
            part = jnp.dot(left, g_ref[:, cols], preferred_element_type=f32)
        part = part.astype(bf16)
        outs[0][r : r + step, :] = part[:, :lanes]
        outs[1][r : r + step, :] = part[:, lanes:]


def all_grads(core_ref, first, second, g_ref, outs, pairs):
    def body(a, b):
        for n, pair in enumerate(pairs):
            both = outs[4 * n : 4 * n + 2], outs[4 * n + 2 : 4 * n + 4]
            of_a, of_b = both if a is first else both[::-1]
            grad_blocks(b, g_ref, of_a, pair, True)
            grad_blocks(a, g_ref, of_b, pair, False)

    by_core(core_ref, body, first, second)


def first_kernel(batch, core_ref, *refs):
    first_view, second_view = refs[:8], refs[8:16]
    main, loss_main, mine, recv = refs[16:20]
    outs = refs[20:24]
    g_ref, loss_ref = refs[24:]
    size = 7 * lanes
    g_ref[:size, :size] = main[...]
    total = jnp.zeros((8, lanes), f32)
    for n in range(15):
        rows = slice(n * lanes, (n + 1) * lanes)
        both = mine[rows, :].astype(f32) + recv[rows, :].astype(f32)
        total = total + squares(both)
        both = (both * (2.0 * off_weight / batch)).astype(bf16)
        if n < 8:
            g_ref[size:, rows] = both
        else:
            g_ref[(n - 8) * lanes : (n - 7) * lanes, size:] = both
    total = loss_main[...] + total * (off_weight / (batch * batch))
    total = jnp.sum(total, axis=0, keepdims=True)
    high = total.astype(bf16)
    total = total - high.astype(f32)
    mid = total.astype(bf16)
    low = (total - mid.astype(f32)).astype(bf16)
    loss_ref[...] = jnp.concatenate(
        [high, mid, low, jnp.zeros((loss_rows - 3, lanes), bf16)], axis=0
    )
    all_grads(core_ref, first_view, second_view, g_ref, outs, (3,))


def rest_kernel(core_ref, *refs):
    first, second, g_ref, outs = refs[:8], refs[8:16], refs[16], refs[17:]
    all_grads(core_ref, first, second, g_ref, outs, (2, 1, 0))


def add_kernel(count, sums, *refs):
    for n, out in enumerate(refs[-sums:]):
        terms = refs[count * n : count * n + count]
        out[...] = sum(t[...].astype(f32) for t in terms).astype(bf16)


def sums_kernel(x_ref, mine_ref, other_ref, diag_ref, *refs):
    parts_1, parts_2 = refs[:4], refs[4:8]
    full_ref, sums_ref = refs[8:]
    rows = x_ref.shape[0]
    mean, rstd = merge_stats(mine_ref[...], other_ref[...], rows)
    norm = (x_ref[...].astype(f32) - mean) * rstd
    rounded = norm.astype(bf16).astype(f32)
    coef = -2.0 * (1.0 - diag_ref[0:1, :])
    first = sum(p[...].astype(f32) for p in parts_1) + coef * rounded[:, lanes:]
    second = sum(p[...].astype(f32) for p in parts_2) + coef * rounded[:, :lanes]
    full = jnp.concatenate([first, second], axis=1)
    full_ref[...] = full
    s1 = jnp.sum(full, axis=0, keepdims=True)
    s2 = jnp.sum(full * norm, axis=0, keepdims=True)
    sums_ref[...] = jnp.concatenate([s1, s2, jnp.zeros((6, 2 * lanes), f32)], axis=0)


def final_kernel(x_ref, mine_ref, other_ref, full_ref, s_mine, s_other, loss_ref, out_ref):
    rows = x_ref.shape[0]
    groups = out_ref.shape[0]
    share = rows // groups
    mean, rstd = merge_stats(mine_ref[...], other_ref[...], rows)
    norm = (x_ref[...].astype(f32) - mean) * rstd
    other = s_other[...]
    other = jnp.concatenate([other[:, lanes:], other[:, :lanes]], axis=1)
    sums = (s_mine[...] + other) / (2 * rows)
    grad = (rstd * (full_ref[...] - sums[0:1] - norm * sums[1:2])).astype(bf16)
    grad = grad.reshape(groups, share, 2 * lanes)
    out_ref[:, :share, :] = grad[:, :, :lanes]
    out_ref[:, share : 2 * share, :] = grad[:, :, lanes:]
    loss = loss_ref[...][None]
    out_ref[:, 2 * share :, :] = jnp.broadcast_to(loss, (groups,) + loss_ref.shape)


def rows_kernel(core_ref, x_ref, a_ref, b_ref, loss_ref):
    share = a_ref.shape[0]

    def body(a, b):
        for g in range(x_ref.shape[0]):
            cols = slice(g * lanes, (g + 1) * lanes)
            a[:, cols] = x_ref[g, :share, :]
            b[:, cols] = x_ref[g, share : 2 * share, :]

    by_core(core_ref, body, a_ref, b_ref)
    loss = jnp.sum(x_ref[:, 2 * share :, :].astype(f32), axis=0)
    loss_ref[0, 0] = jnp.sum(loss) * (1.0 / a_ref.shape[1])


def gather(own, role):
    side, left, right = across(own, role), line(own, role, 1), line(own, role, -1)
    if role == 0:
        side, left, right = gate(side, left, right)
        side_left, side_right = line(side, role, 1), across(right, role)
        opposite = line(right, role, -1)
        last = line(side_left, role, 1)
    else:
        left, right = gate(left, right)
        side_right = across(right, role)
        last = line(side_right, role, -1)
        side, far = gate(side, right)
        side_left, opposite = line(side, role, 1), line(far, role, -1)
    return [own, side, left, right, side_left, side_right, opposite, last]


def on_device(view_a, view_b):
    rows_dev, features = view_a.shape
    groups = features // lanes
    rows = rows_dev * groups
    batch = 2 * rows
    block = shape((rows, lanes), bf16)
    core = lax.axis_index("c").astype(jnp.int32)
    core_0 = core == 0

    def split(view):
        return view.reshape(rows_dev, groups, lanes).transpose(1, 0, 2)

    a, b = split(view_a), split(view_b)
    both = jnp.concatenate([jnp.where(core_0, a, b), jnp.where(core_0, b, a)], axis=2)
    x = lax.all_to_all(both, chips, 0, 0, tiled=True).reshape(rows, 2 * lanes)
    mine = call(stats_kernel, shape((8, 2 * lanes), f32), x)
    other = swap(mine)
    own_1, own_2, diag_mine = call(
        norm_kernel, (block, block, shape((8, lanes), f32)), x, mine, other
    )
    diag_other = swap(diag_mine)
    views = [*gather(own_1, 0), *gather(own_2, 1)]
    size = 8 * lanes
    work = 2 * rows * size * size
    place = core.reshape(1)
    main = 7 * lanes
    corr_mine = call(
        corr_kernel,
        shape((main, main), bf16),
        place,
        *views[:7],
        *views[8:15],
        scratch=[pltpu.VMEM((main, rows), bf16)],
        flops=work * 3 // 4,
        scalar=True,
    )
    g_main, loss_main, diag = call(
        functools.partial(main_g_kernel, batch),
        (shape((main, main), bf16), shape((8, lanes), f32), shape((8, lanes), f32)),
        corr_mine,
        swap(*gate(corr_mine, others=(views[7], views[15]))),
        diag_mine,
        diag_other,
    )
    last_mine = call(
        corr_last_kernel,
        shape((15 * lanes, lanes), bf16),
        place,
        *views,
        flops=work // 4,
        scalar=True,
    )
    *far, g, loss = call(
        functools.partial(first_kernel, batch),
        (block,) * 4 + (shape((size, size), bf16), shape((loss_rows, lanes), bf16)),
        place,
        *views,
        g_main,
        loss_main,
        last_mine,
        swap(last_mine),
        flops=work // 2,
        scalar=True,
    )
    last_in = line(far[1], 0, -1), line(far[3], 1, 1)
    far_in = line(far[0], 0, 1), line(far[2], 1, 1)
    rest = call(
        rest_kernel, (block,) * 12, place, *views, g, flops=work * 3 // 2, scalar=True
    )

    def add(count, *terms, others=()):
        n = len(terms) // count
        return call(functools.partial(add_kernel, count, n), (block,) * n, *terms, *others)

    side_left, side_right = rest[0:4:2], rest[1:4:2]
    left, right, own, side = rest[4:8:2], rest[5:8:2], rest[8:12:2], rest[9:12:2]
    (sum_1,) = add(2, side_left[0], last_in[0])
    (sum_2,) = add(2, side_right[1], last_in[1], others=far_in[:1])
    side_left, side_right = (sum_1, side_left[1]), (side_right[0], sum_2)
    side_in = [line(v, n, -1) for n, v in enumerate(side_left)]
    right_in = [across(v, n) for n, v in enumerate(side_right)]
    parts = []
    for n in range(2):
        (right_sum,) = add(3, right[n], right_in[n], far_in[n])
        (side_sum,) = add(2, side[n], side_in[n])
        parts += [own[n], line(left[n], n, -1), line(right_sum, n, 1), across(side_sum, n)]
    full, s_mine = call(
        sums_kernel,
        (shape((rows, 2 * lanes), f32), shape((8, 2 * lanes), f32)),
        x,
        mine,
        other,
        diag,
        *parts,
    )
    s_other = swap(s_mine)
    grads = call(
        final_kernel,
        shape((groups, 2 * rows_dev + loss_rows, lanes), bf16),
        x,
        mine,
        other,
        full,
        s_mine,
        s_other,
        loss,
    )
    back = lax.all_to_all(grads, chips, 0, 0, tiled=True)
    grad_a, grad_b, total = call(
        rows_kernel,
        (*[shape((rows_dev, features), bf16)] * 2, shape((1, 1), f32)),
        place,
        back,
        scalar=True,
        last_scalar=True,
    )
    return (total.reshape(()), grad_a, grad_b)


def solution(mesh):
    split = Mesh(mesh.devices.reshape(sizes), axes)
    return jax.shard_map(
        on_device,
        mesh=split,
        in_specs=(P(axes, None), P(axes, None)),
        out_specs=(P(), P(axes, None), P(axes, None)),
        check_vma=False,
    )
```

```python
import functools

import jax
import jax.numpy as jnp
from jax import lax
from jax.experimental import pallas as pl
from jax.experimental.pallas import tpu as pltpu
from jax.sharding import Mesh, PartitionSpec as P

off_weight = 0.0051
norm_eps = 1e-05
bf16 = jnp.bfloat16
f32 = jnp.float32
axes = ("z", "x", "y", "c")
chips = ("x", "y", "z")
sizes = (4, 4, 4, 2)
lanes = 128
vmem_limit = 24 * 2**20
half = 2048
loss_rows = 8


def call(kernel, out_shape, *args, scratch=(), flops=0, scalar=False, last_scalar=False):
    one = isinstance(out_shape, jax.ShapeDtypeStruct)
    outs = [out_shape] if one else list(out_shape)
    vmem = pl.BlockSpec(memory_space=pltpu.VMEM)
    specs = [vmem] * len(args)
    if scalar:
        specs[0] = pl.BlockSpec(memory_space=pltpu.SMEM)
    out_specs = [vmem] * len(outs)
    if last_scalar:
        out_specs[-1] = pl.BlockSpec(memory_space=pltpu.SMEM)
    traffic = sum(a.size * a.dtype.itemsize for a in list(args) + outs)
    return pl.pallas_call(
        kernel,
        out_shape=out_shape,
        in_specs=specs,
        out_specs=vmem if one else out_specs,
        scratch_shapes=list(scratch),
        compiler_params=pltpu.CompilerParams(vmem_limit_bytes=vmem_limit),
        cost_estimate=pl.CostEstimate(flops=flops, bytes_accessed=traffic, transcendentals=0),
    )(*args)


def shape(dims, dtype):
    return jax.ShapeDtypeStruct(dims, dtype)


def device(z, x, y, c):
    return ((z * 4 + x) * 4 + y) * 2 + c


def moved(target):
    places = [(z, x, y, c) for z in range(4) for x in range(4) for y in range(4) for c in range(2)]
    return [(device(*p), device(*target(*p))) for p in places]


def line(x, role, step):
    def target(z, x, y, c):
        return (z, x, (y + step) % 4, c) if c == role else ((z + step) % 4, x, y, c)

    return lax.ppermute(x, axes, moved(target))


def across(x, role):
    def target(z, x, y, c):
        return (z, x ^ 1 if c == role else 3 - x, y, c)

    return lax.ppermute(x, axes, moved(target))


def swap(x):
    return lax.ppermute(x, axes, moved(lambda z, x, y, c: (z, x, y, 1 - c)))


def gate_kernel(n, *refs):
    for x, out in zip(refs[:n], refs[-n:]):
        out[...] = x[...]


def gate(*xs, others=()):
    outs = [shape(x.shape, x.dtype) for x in xs]
    return call(functools.partial(gate_kernel, len(xs)), outs, *xs, *others)


def stats_kernel(x_ref, out_ref):
    x = x_ref[...].astype(f32)
    mean = jnp.mean(x, axis=0, keepdims=True)
    centred = x - mean
    m2 = jnp.sum(centred * centred, axis=0, keepdims=True)
    width = x.shape[1]
    out_ref[...] = jnp.concatenate([mean, m2, jnp.zeros((6, width), f32)], axis=0)


def merge_stats(mine, other, rows):
    other = jnp.concatenate([other[:, lanes:], other[:, :lanes]], axis=1)
    delta = other[0:1] - mine[0:1]
    mean = 0.5 * (mine[0:1] + other[0:1])
    var = (mine[1:2] + other[1:2]) / (2 * rows) + 0.25 * delta * delta
    return mean, lax.rsqrt(var + norm_eps)


def norm_kernel(x_ref, mine_ref, other_ref, a_ref, b_ref, diag_ref):
    rows = x_ref.shape[0]
    mean, rstd = merge_stats(mine_ref[...], other_ref[...], rows)
    norm = ((x_ref[...].astype(f32) - mean) * rstd).astype(bf16)
    a = norm[:, :lanes]
    b = norm[:, lanes:]
    a_ref[...] = a
    b_ref[...] = b
    diag = jnp.sum(a.astype(f32) * b.astype(f32), axis=0, keepdims=True)
    diag_ref[...] = jnp.broadcast_to(diag, diag_ref.shape)


def by_core(core_ref, body, first, second):
    @pl.when(core_ref[0] == 0)
    def _():
        body(first, second)

    @pl.when(core_ref[0] != 0)
    def _():
        body(second, first)


def corr_kernel(core_ref, *refs):
    first, second, out_ref, a_t = refs[:7], refs[7:14], refs[14], refs[15]

    def body(a, b):
        for i in range(7):
            a_t[i * lanes : (i + 1) * lanes, :] = a[i][...].T
        for q in range(0, 7, 2):
            right = jnp.concatenate([v[...] for v in b[q : q + 2]], axis=1)
            cols = slice(q * lanes, min(q + 2, 7) * lanes)
            for p in range(0, 7, 2):
                here = slice(p * lanes, min(p + 2, 7) * lanes)
                out_ref[here, cols] = jnp.dot(
                    a_t[here, :], right, preferred_element_type=f32
                ).astype(bf16)

    by_core(core_ref, body, first, second)


def corr_last_kernel(core_ref, *refs):
    first, second, out_ref = refs[:8], refs[8:16], refs[16]

    def body(a, b):
        a_t = a[7][...].T
        b_t = b[7][...].T
        for q in range(0, 8, 2):
            right = jnp.concatenate([b[q][...], b[q + 1][...]], axis=1)
            part = jnp.dot(a_t, right, preferred_element_type=f32).astype(bf16)
            out_ref[q * lanes : (q + 1) * lanes, :] = part[:, :lanes]
            out_ref[(q + 1) * lanes : (q + 2) * lanes, :] = part[:, lanes:]
        for p in range(0, 8, 2):
            right = jnp.concatenate([a[p][...], a[p + 1][...]], axis=1)
            part = jnp.dot(b_t, right, preferred_element_type=f32)
            for n in range(p, min(p + 2, 7)):
                block = part[:, (n - p) * lanes : (n - p + 1) * lanes].T
                out_ref[(8 + n) * lanes : (9 + n) * lanes, :] = block.astype(bf16)

    by_core(core_ref, body, first, second)


def main_g_kernel(batch, mine, recv, diag_mine, diag_recv, g_ref, loss_ref, diag_ref):
    size = mine.shape[0]
    diag = (diag_mine[...] + diag_recv[...]) * (1.0 / batch)
    diag_ref[...] = diag
    missing = 1.0 - diag
    first = lax.broadcasted_iota(jnp.int32, (8, lanes), 0) == 0
    total = jnp.zeros((8, lanes), f32)
    for r in range(0, size, lanes):
        both = mine[r : r + lanes, :].astype(f32) + recv[r : r + lanes, :].astype(f32)
        if r == 0:
            ids = lax.broadcasted_iota(jnp.int32, (lanes, size), 0)
            same = ids == lax.broadcasted_iota(jnp.int32, (lanes, size), 1)
            both = jnp.where(same, 0.0, both)
        g_ref[r : r + lanes, :] = (both * (2.0 * off_weight / batch)).astype(bf16)
        total = total + squares(both)
    total = total * (off_weight / (batch * batch))
    loss_ref[...] = total + jnp.where(first, missing * missing, 0.0)


def squares(x):
    square = jnp.sum((x * x).reshape(x.shape[0] // 8, 8, x.shape[1]), axis=0)
    return sum(square[:, c : c + lanes] for c in range(0, x.shape[1], lanes))


def grad_blocks(b, g_ref, outs, pair, transposed):
    cols = slice(pair * 256, (pair + 1) * 256)
    step = 256
    for r in range(0, half, step):
        left = jnp.concatenate([v[r : r + step, :] for v in b], axis=1)
        if transposed:
            part = lax.dot_general(
                left, g_ref[cols, :], (((1,), (1,)), ((), ())), preferred_element_type=f32
            )
        else:
            part = jnp.dot(left, g_ref[:, cols], preferred_element_type=f32)
        part = part.astype(bf16)
        outs[0][r : r + step, :] = part[:, :lanes]
        outs[1][r : r + step, :] = part[:, lanes:]


def all_grads(core_ref, first, second, g_ref, outs, pairs):
    def body(a, b):
        for n, pair in enumerate(pairs):
            both = outs[4 * n : 4 * n + 2], outs[4 * n + 2 : 4 * n + 4]
            of_a, of_b = both if a is first else both[::-1]
            grad_blocks(b, g_ref, of_a, pair, True)
            grad_blocks(a, g_ref, of_b, pair, False)

    by_core(core_ref, body, first, second)


def first_kernel(batch, core_ref, *refs):
    first_view, second_view = refs[:8], refs[8:16]
    main, loss_main, mine, recv = refs[16:20]
    outs = refs[20:24]
    g_ref, loss_ref = refs[24:]
    size = 7 * lanes
    g_ref[:size, :size] = main[...]
    total = jnp.zeros((8, lanes), f32)
    for n in range(15):
        rows = slice(n * lanes, (n + 1) * lanes)
        both = mine[rows, :].astype(f32) + recv[rows, :].astype(f32)
        total = total + squares(both)
        both = (both * (2.0 * off_weight / batch)).astype(bf16)
        if n < 8:
            g_ref[size:, rows] = both
        else:
            g_ref[(n - 8) * lanes : (n - 7) * lanes, size:] = both
    total = loss_main[...] + total * (off_weight / (batch * batch))
    total = jnp.sum(total, axis=0, keepdims=True)
    high = total.astype(bf16)
    total = total - high.astype(f32)
    mid = total.astype(bf16)
    low = (total - mid.astype(f32)).astype(bf16)
    loss_ref[...] = jnp.concatenate(
        [high, mid, low, jnp.zeros((loss_rows - 3, lanes), bf16)], axis=0
    )
    all_grads(core_ref, first_view, second_view, g_ref, outs, (3,))


def rest_kernel(core_ref, *refs):
    first, second, g_ref, outs = refs[:8], refs[8:16], refs[16], refs[17:]
    all_grads(core_ref, first, second, g_ref, outs, (2, 1, 0))


def add_kernel(count, sums, *refs):
    for n, out in enumerate(refs[-sums:]):
        terms = refs[count * n : count * n + count]
        out[...] = sum(t[...].astype(f32) for t in terms).astype(bf16)


def sums_kernel(x_ref, mine_ref, other_ref, diag_ref, *refs):
    parts_1, parts_2 = refs[:4], refs[4:8]
    full_ref, sums_ref = refs[8:]
    rows = x_ref.shape[0]
    mean, rstd = merge_stats(mine_ref[...], other_ref[...], rows)
    norm = (x_ref[...].astype(f32) - mean) * rstd
    rounded = norm.astype(bf16).astype(f32)
    coef = -2.0 * (1.0 - diag_ref[0:1, :])
    first = sum(p[...].astype(f32) for p in parts_1) + coef * rounded[:, lanes:]
    second = sum(p[...].astype(f32) for p in parts_2) + coef * rounded[:, :lanes]
    full = jnp.concatenate([first, second], axis=1)
    full_ref[...] = full
    s1 = jnp.sum(full, axis=0, keepdims=True)
    s2 = jnp.sum(full * norm, axis=0, keepdims=True)
    sums_ref[...] = jnp.concatenate([s1, s2, jnp.zeros((6, 2 * lanes), f32)], axis=0)


def final_kernel(x_ref, mine_ref, other_ref, full_ref, s_mine, s_other, loss_ref, out_ref):
    rows = x_ref.shape[0]
    groups = out_ref.shape[0]
    share = rows // groups
    mean, rstd = merge_stats(mine_ref[...], other_ref[...], rows)
    norm = (x_ref[...].astype(f32) - mean) * rstd
    other = s_other[...]
    other = jnp.concatenate([other[:, lanes:], other[:, :lanes]], axis=1)
    sums = (s_mine[...] + other) / (2 * rows)
    grad = (rstd * (full_ref[...] - sums[0:1] - norm * sums[1:2])).astype(bf16)
    grad = grad.reshape(groups, share, 2 * lanes)
    out_ref[:, :share, :] = grad[:, :, :lanes]
    out_ref[:, share : 2 * share, :] = grad[:, :, lanes:]
    loss = loss_ref[...][None]
    out_ref[:, 2 * share :, :] = jnp.broadcast_to(loss, (groups,) + loss_ref.shape)


def rows_kernel(core_ref, x_ref, a_ref, b_ref, loss_ref):
    share = a_ref.shape[0]

    def body(a, b):
        for g in range(x_ref.shape[0]):
            cols = slice(g * lanes, (g + 1) * lanes)
            a[:, cols] = x_ref[g, :share, :]
            b[:, cols] = x_ref[g, share : 2 * share, :]

    by_core(core_ref, body, a_ref, b_ref)
    loss = jnp.sum(x_ref[:, 2 * share :, :].astype(f32), axis=0)
    loss_ref[0, 0] = jnp.sum(loss) * (1.0 / a_ref.shape[1])


def gather(own, role):
    side, left, right = across(own, role), line(own, role, 1), line(own, role, -1)
    if role == 0:
        side, left, right = gate(side, left, right)
        side_left, side_right = line(side, role, 1), across(right, role)
        opposite = line(right, role, -1)
        last = line(side_left, role, 1)
    else:
        left, right = gate(left, right)
        side_right = across(right, role)
        last = line(side_right, role, -1)
        side, far = gate(side, right)
        side_left, opposite = line(side, role, 1), line(far, role, -1)
    return [own, side, left, right, side_left, side_right, opposite, last]


def on_device(view_a, view_b):
    rows_dev, features = view_a.shape
    groups = features // lanes
    rows = rows_dev * groups
    batch = 2 * rows
    block = shape((rows, lanes), bf16)
    core = lax.axis_index("c").astype(jnp.int32)
    core_0 = core == 0

    def split(view):
        return view.reshape(rows_dev, groups, lanes).transpose(1, 0, 2)

    a, b = split(view_a), split(view_b)
    both = jnp.concatenate([jnp.where(core_0, a, b), jnp.where(core_0, b, a)], axis=2)
    x = lax.all_to_all(both, chips, 0, 0, tiled=True).reshape(rows, 2 * lanes)
    mine = call(stats_kernel, shape((8, 2 * lanes), f32), x)
    other = swap(mine)
    own_1, own_2, diag_mine = call(
        norm_kernel, (block, block, shape((8, lanes), f32)), x, mine, other
    )
    diag_other = swap(diag_mine)
    views = [*gather(own_1, 0), *gather(own_2, 1)]
    size = 8 * lanes
    work = 2 * rows * size * size
    place = core.reshape(1)
    main = 7 * lanes
    corr_mine = call(
        corr_kernel,
        shape((main, main), bf16),
        place,
        *views[:7],
        *views[8:15],
        scratch=[pltpu.VMEM((main, rows), bf16)],
        flops=work * 3 // 4,
        scalar=True,
    )
    g_main, loss_main, diag = call(
        functools.partial(main_g_kernel, batch),
        (shape((main, main), bf16), shape((8, lanes), f32), shape((8, lanes), f32)),
        corr_mine,
        swap(*gate(corr_mine, others=(views[7], views[15]))),
        diag_mine,
        diag_other,
    )
    last_mine = call(
        corr_last_kernel,
        shape((15 * lanes, lanes), bf16),
        place,
        *views,
        flops=work // 4,
        scalar=True,
    )
    *far, g, loss = call(
        functools.partial(first_kernel, batch),
        (block,) * 4 + (shape((size, size), bf16), shape((loss_rows, lanes), bf16)),
        place,
        *views,
        g_main,
        loss_main,
        last_mine,
        swap(last_mine),
        flops=work // 2,
        scalar=True,
    )
    last_in = line(far[1], 0, -1), line(far[3], 1, 1)
    far_in = line(far[0], 0, 1), line(far[2], 1, 1)
    rest = call(
        rest_kernel, (block,) * 12, place, *views, g, flops=work * 3 // 2, scalar=True
    )

    def add(count, *terms, others=()):
        n = len(terms) // count
        return call(functools.partial(add_kernel, count, n), (block,) * n, *terms, *others)

    side_left, side_right = rest[0:4:2], rest[1:4:2]
    left, right, own, side = rest[4:8:2], rest[5:8:2], rest[8:12:2], rest[9:12:2]
    (sum_1,) = add(2, side_left[0], last_in[0])
    (sum_2,) = add(2, side_right[1], last_in[1])
    side_left, side_right = (sum_1, side_left[1]), (side_right[0], sum_2)
    side_in = [line(v, n, -1) for n, v in enumerate(side_left)]
    right_in = [across(v, n) for n, v in enumerate(side_right)]
    parts = []
    for n in range(2):
        (right_sum,) = add(3, right[n], right_in[n], far_in[n])
        (side_sum,) = add(2, side[n], side_in[n])
        parts += [own[n], line(left[n], n, -1), line(right_sum, n, 1), across(side_sum, n)]
    full, s_mine = call(
        sums_kernel,
        (shape((rows, 2 * lanes), f32), shape((8, 2 * lanes), f32)),
        x,
        mine,
        other,
        diag,
        *parts,
    )
    s_other = swap(s_mine)
    grads = call(
        final_kernel,
        shape((groups, 2 * rows_dev + loss_rows, lanes), bf16),
        x,
        mine,
        other,
        full,
        s_mine,
        s_other,
        loss,
    )
    back = lax.all_to_all(grads, chips, 0, 0, tiled=True)
    grad_a, grad_b, total = call(
        rows_kernel,
        (*[shape((rows_dev, features), bf16)] * 2, shape((1, 1), f32)),
        place,
        back,
        scalar=True,
        last_scalar=True,
    )
    return (total.reshape(()), grad_a, grad_b)


def solution(mesh):
    split = Mesh(mesh.devices.reshape(sizes), axes)
    return jax.shard_map(
        on_device,
        mesh=split,
        in_specs=(P(axes, None), P(axes, None)),
        out_specs=(P(), P(axes, None), P(axes, None)),
        check_vma=False,
    )
```
